32 devices in a mesh: dp: 8 (over y, x, core), seq: 4 (over z).
Axes of the slice: x: 2, y: 2, z: 4, core: 2. Of those that a mesh axis runs over, the one named last changes fastest.
Arguments:
- tokens: bfloat16 [16384, 1024], P(('dp', 'seq')), may hold values from -6 to 6
- patches: bfloat16 [8192, 1024], P(('dp', 'seq')), may hold values from -6 to 6
- cameras: bfloat16 [32, 16], P('dp'), may hold values from -4 to 4
- tri_items: int32 [16384], P('dp'), may hold values from 0 to 3, as said below
- patch_items: int32 [8192], P('dp'), may hold values from 0 to 3, as said below
- mod_weight: bfloat16 [2048, 16], P(('dp', 'seq')), may hold values from -0.75 to 0.75
- qkv_weight: bfloat16 [1024, 3072], P(('dp', 'seq')), may hold values from -0.1875 to 0.1875
- self_out_weight: bfloat16 [1024, 1024], P(('dp', 'seq')), may hold values from -3 to 3
- norm2_gain: bfloat16 [1024], P(('dp', 'seq')), may hold values from 0.5 to 1.5
- norm2_bias: bfloat16 [1024], P(('dp', 'seq')), may hold values from -3 to 3
- cross_q_weight: bfloat16 [1024, 1024], P(('dp', 'seq')), may hold values from -0.1875 to 0.1875
- cross_kv_weight: bfloat16 [1024, 2048], P(('dp', 'seq')), may hold values from -0.1875 to 0.1875
- cross_out_weight: bfloat16 [1024, 1024], P(('dp', 'seq')), may hold values from -3 to 3
- norm3_gain: bfloat16 [1024], P(('dp', 'seq')), may hold values from 0.5 to 1.5
- norm3_bias: bfloat16 [1024], P(('dp', 'seq')), may hold values from -3 to 3
- mlp_in_weight: bfloat16 [1024, 4096], P(('dp', 'seq')), may hold values from -0.1875 to 0.1875
- mlp_in_bias: bfloat16 [4096], P(('dp', 'seq')), may hold values from -3 to 3
- mlp_out_weight: bfloat16 [4096, 1024], P(('dp', 'seq')), may hold values from -0.09375 to 0.09375
- mlp_out_bias: bfloat16 [1024], P(('dp', 'seq')), may hold values from -3 to 3
- cotangent: bfloat16 [16384, 1024], P(('dp', 'seq')), may hold values from -6 to 6
Outputs:
- block_out: bfloat16 [16384, 1024], P(('dp', 'seq'))
- input_grad: float32 [16384, 1024], P(('dp', 'seq'))
- patch_grad: float32 [8192, 1024], P(('dp', 'seq'))
- mod_weight_grad: float32 [2048, 16], P(('dp', 'seq'))
- qkv_weight_grad: float32 [1024, 3072], P(('dp', 'seq'))
- self_out_weight_grad: float32 [1024, 1024], P(('dp', 'seq'))
- norm2_gain_grad: float32 [1024], P(('dp', 'seq'))
- norm2_bias_grad: float32 [1024], P(('dp', 'seq'))
- cross_q_weight_grad: float32 [1024, 1024], P(('dp', 'seq'))
- cross_kv_weight_grad: float32 [1024, 2048], P(('dp', 'seq'))
- cross_out_weight_grad: float32 [1024, 1024], P(('dp', 'seq'))
- norm3_gain_grad: float32 [1024], P(('dp', 'seq'))
- norm3_bias_grad: float32 [1024], P(('dp', 'seq'))
- mlp_in_weight_grad: float32 [1024, 4096], P(('dp', 'seq'))
- mlp_in_bias_grad: float32 [4096], P(('dp', 'seq'))
- mlp_out_weight_grad: float32 [4096, 1024], P(('dp', 'seq'))
- mlp_out_bias_grad: float32 [1024], P(('dp', 'seq'))
The draws below stay inside these ranges and needn't reach their ends.
Inputs may be any that keep to these rules, and one draw needn't show every extreme that they name: `tri_items`: within each group item numbers never fall along the rows, every item has tokens, and one item of each group, drawn from the seed, runs from the group's first 512 rows into its last 512 rows. `patch_items`: within each group item numbers never fall along the rows and every item has patches.
All inputs are finite; a program needn't handle non-finite values.
Results may differ from the reference program's by a relative error of at most 0.017.
Values may be sent and summed in bfloat16 or wider, within the bound.
No kernel may reach another device: no remote copies, remote signals or barrier semaphores. Data moves between devices by JAX's collectives and lax.ppermute only.
A program may use at most 320 MiB of HBM per device.

```python
import math
import jax
import jax.numpy as jnp
from jax import lax

D = 1024
HEADS = 16
FF = 4096
CAM = 16
ITEM_GROUP = 4
TRI_DEV = 512
PATCH_DEV = 256
TOKENS = 16384
PATCHES = 8192
ITEMS = 32
N_DP = 8
N_SEQ = 4


def segment_ids(key, block, span):
    keys = jax.random.split(key, N_DP)
    step_size = block // ITEM_GROUP
    jitter_top = max(step_size // 2, 1)

    def one_group(group_key):
        first_key, second_key = jax.random.split(group_key)
        before = jax.random.randint(first_key, (), 0, ITEM_GROUP)
        jitter = jax.random.randint(second_key, (ITEM_GROUP - 1,), 0, jitter_top)
        index = jnp.arange(1, ITEM_GROUP, dtype=jnp.int32)
        early = index * step_size - jitter
        late = span - block + (index - before) * step_size - jitter
        cuts = jnp.where(index <= before, early, late)
        where_pos = jnp.arange(span, dtype=jnp.int32)
        return jnp.sum((where_pos[:, None] >= cuts[None, :]).astype(jnp.int32), axis=1)
    return jax.vmap(one_group)(keys).reshape(N_DP * span)


def draw_tri_items(key, part):
    key = jax.random.fold_in(key, 11)
    return segment_ids(key, TRI_DEV, TRI_DEV * N_SEQ)


def draw_patch_items(key, part):
    key = jax.random.fold_in(key, 23)
    return segment_ids(key, PATCH_DEV, PATCH_DEV * N_SEQ)


def steps_of(own_key, shape, cuts, smallest, largest):
    def one(dim, blocks):
        heights = jax.random.uniform(jax.random.fold_in(jax.random.fold_in(own_key, 6), dim), (blocks,), jnp.float32, smallest / len(cuts), largest / len(cuts))
        return jnp.repeat(jnp.exp(heights), shape[dim] // blocks).reshape((-1,) + (1,) * (len(shape) - dim - 1))

    gain = one(*cuts[0])
    for cut in cuts[1:]:
        gain = gain * one(*cut)
    return gain


def noise(key, dims, scale, bound, cuts=(), kind=jnp.bfloat16):
    drawn = scale * jax.random.normal(key, dims, jnp.float32)
    if cuts:
        drawn = drawn * steps_of(key, dims, cuts, -0.22, 0.18)
    return jnp.clip(drawn, -bound, bound).astype(kind)


def setup_inputs(seed: int = 0) -> dict:
    streams_of = jax.random.split(jax.random.key(seed), 21)
    return {
        "tokens": noise(streams_of[0], (TOKENS, D), 1.0, 6.0, ((0, 32),)),
        "patches": noise(streams_of[1], (PATCHES, D), 1.0, 6.0, ((0, 32),)),
        "cameras": noise(streams_of[2], (ITEMS, CAM), 1.0, 4.0, ((0, 8),)),
        "tri_items": draw_tri_items(jax.random.fold_in(streams_of[20], 71), 0),
        "patch_items": draw_patch_items(jax.random.fold_in(streams_of[20], 71), 0),
        "mod_weight": noise(streams_of[5], (2 * D, CAM), (4 * CAM) ** -0.5, 0.75, ((0, 32),)),
        "qkv_weight": noise(streams_of[6], (D, 3 * D), D ** -0.5, 0.1875, ((0, 32),)),
        "self_out_weight": noise(streams_of[7], (D, D), (max(D // 256, 1)) ** -0.5, 3.0, ((0, 32),)),
        "norm2_gain": jnp.clip(1.0 + 0.1 * jax.random.normal(streams_of[8], (D,), jnp.float32), 0.5, 1.5).astype(jnp.bfloat16),
        "norm2_bias": noise(streams_of[9], (D,), 0.3, 3.0, ((0, 32),)),
        "cross_q_weight": noise(streams_of[10], (D, D), D ** -0.5, 0.1875, ((0, 32),)),
        "cross_kv_weight": noise(streams_of[11], (D, 2 * D), D ** -0.5, 0.1875, ((0, 32),)),
        "cross_out_weight": noise(streams_of[12], (D, D), (max(D // 256, 1)) ** -0.5, 3.0, ((0, 32),)),
        "norm3_gain": jnp.clip(1.0 + 0.1 * jax.random.normal(streams_of[13], (D,), jnp.float32), 0.5, 1.5).astype(jnp.bfloat16),
        "norm3_bias": noise(streams_of[14], (D,), 0.3, 3.0, ((0, 32),)),
        "mlp_in_weight": noise(streams_of[15], (D, FF), D ** -0.5, 0.1875, ((0, 32),)),
        "mlp_in_bias": noise(streams_of[16], (FF,), 0.3, 3.0, ((0, 32),)),
        "mlp_out_weight": noise(streams_of[17], (FF, D), FF ** -0.5, 0.09375, ((0, 32),)),
        "mlp_out_bias": noise(streams_of[18], (D,), 0.3, 3.0, ((0, 32),)),
        "cotangent": noise(streams_of[19], (TOKENS, D), 1.0, 6.0, ((0, 32),)),
    }


@jax.custom_vjp
def low(v):
    return lax.optimization_barrier(v.astype(jnp.bfloat16)).astype(jnp.float32)

@jax.custom_vjp
def low_back(v):
    return v

def low_keep(v):
    return (low(v), None)

def low_pass(kept, grad):
    return (grad,)

def back_keep(v):
    return (v, None)

def back_low(kept, grad):
    return (low(grad),)
low.defvjp(low_keep, low_pass)
low_back.defvjp(back_keep, back_low)

def matmul(left_side, right_side):
    return jnp.dot(left_side, right_side, precision=lax.Precision.HIGHEST)

def normed(values):
    centre = values - lax.optimization_barrier(jnp.mean(values, axis=-1, keepdims=True))
    spread = lax.optimization_barrier(jnp.mean(centre * centre, axis=-1, keepdims=True))
    return centre * lax.rsqrt(spread + 1e-05)

def attention(queries, key_rows, values, query_ids, key_ids):
    head_dim = D // HEADS
    score_scale = 1.0 / math.sqrt(head_dim)
    allowed = query_ids[:, None] == key_ids[None, :]

    def split_heads(tensor):
        return tensor.reshape(tensor.shape[0], HEADS, head_dim).transpose(1, 0, 2)

    def one_head(pieces):
        head_q, head_k, head_v = pieces
        scores = low_back(matmul(head_q, head_k.T) * score_scale)
        scores = jnp.where(allowed, scores, -1e+30)
        row_max = lax.optimization_barrier(jnp.max(scores, axis=1, keepdims=True))
        exponent = jnp.exp(scores - row_max)
        probs_low = low(exponent / lax.optimization_barrier(jnp.sum(exponent, axis=1, keepdims=True)))
        return matmul(probs_low, head_v)
    outputs = lax.map(jax.checkpoint(one_head), (split_heads(queries), split_heads(key_rows), split_heads(values)))
    return outputs.transpose(1, 0, 2).reshape(queries.shape[0], D)

def group_forward(params, token_rows, patch_rows, camera_rows, token_ids, patch_ids):
    mod_w, qkv_w, self_out_w, gain_two, bias_two, cross_q_w, cross_kv_w, cross_out_w, gain_three, bias_three, in_w, in_bias, out_w, out_bias = params
    onehot = (token_ids[:, None] == jnp.arange(ITEM_GROUP, dtype=jnp.int32)[None, :]).astype(jnp.float32)
    mod_tok = matmul(onehot, matmul(camera_rows, mod_w.T))
    shift_tok = mod_tok[:, :D]
    scale_tok = mod_tok[:, D:]
    act_one = low(normed(token_rows) * (1.0 + scale_tok) + shift_tok)
    qkv_all = low_back(low(matmul(act_one, qkv_w)))
    self_att = low_back(low(attention(qkv_all[:, :D], qkv_all[:, D:2 * D], qkv_all[:, 2 * D:], token_ids, token_ids)))
    resid_two = token_rows + low_back(matmul(self_att, self_out_w))
    act_two = low(normed(resid_two) * gain_two + bias_two)
    cross_q = low_back(low(matmul(act_two, cross_q_w)))
    cross_kv = low_back(low(matmul(patch_rows, cross_kv_w)))
    cross_att = low_back(low(attention(cross_q, cross_kv[:, :D], cross_kv[:, D:], token_ids, patch_ids)))
    resid_three = resid_two + low_back(matmul(cross_att, cross_out_w))
    act_three = low(normed(resid_three) * gain_three + bias_three)
    hidden_pre = low_back(matmul(act_three, in_w) + in_bias)
    hidden_low = low(jax.nn.gelu(hidden_pre, approximate=False))
    return resid_three + matmul(hidden_low, out_w) + out_bias

def reference(tokens, patches, cameras, tri_items, patch_items, mod_weight, qkv_weight, self_out_weight, norm2_gain, norm2_bias, cross_q_weight, cross_kv_weight, cross_out_weight, norm3_gain, norm3_bias, mlp_in_weight, mlp_in_bias, mlp_out_weight, mlp_out_bias, cotangent):
    params = tuple((weight.astype(jnp.float32) for weight in (mod_weight, qkv_weight, self_out_weight, norm2_gain, norm2_bias, cross_q_weight, cross_kv_weight, cross_out_weight, norm3_gain, norm3_bias, mlp_in_weight, mlp_in_bias, mlp_out_weight, mlp_out_bias)))
    group_tokens = TOKENS // N_DP
    group_patches = PATCHES // N_DP
    token_groups = tokens.astype(jnp.float32).reshape(N_DP, group_tokens, D)
    patch_groups = patches.astype(jnp.float32).reshape(N_DP, group_patches, D)
    camera_groups = cameras.astype(jnp.float32).reshape(N_DP, ITEM_GROUP, CAM)
    token_id_groups = tri_items.reshape(N_DP, group_tokens)
    patch_id_groups = patch_items.reshape(N_DP, group_patches)

    def forward(weights, token_all, patch_all):

        def one_group(pieces):
            token_rows, patch_rows, camera_rows, token_ids, patch_ids = pieces
            return group_forward(weights, token_rows, patch_rows, camera_rows, token_ids, patch_ids)
        return lax.map(one_group, (token_all, patch_all, camera_groups, token_id_groups, patch_id_groups))
    result, pullback = jax.vjp(forward, params, token_groups, patch_groups)
    weight_grads, token_grads, patch_grads = pullback(cotangent.astype(jnp.float32).reshape(N_DP, group_tokens, D))
    g_mod, g_qkv, g_self_out, g_gain_two, g_bias_two, g_cross_q, g_cross_kv, g_cross_out, g_gain_three, g_bias_three, g_in, g_in_bias, g_out, g_out_bias = weight_grads
    return (result.reshape(TOKENS, D).astype(jnp.bfloat16), token_grads.reshape(TOKENS, D), patch_grads.reshape(PATCHES, D), g_mod, g_qkv, g_self_out, g_gain_two, g_bias_two, g_cross_q, g_cross_kv, g_cross_out, g_gain_three, g_bias_three, g_in, g_in_bias, g_out, g_out_bias)
```

```python
import math

import jax
import jax.numpy as jnp
from jax import lax
from jax.experimental import pallas as pl
from jax.experimental.pallas import tpu as pltpu
from jax.sharding import PartitionSpec as P

HEADS = 16
HEAD = 64
PAIR = 2 * HEAD
BF = jnp.bfloat16
F32 = jnp.float32
LOG2E = math.log2(math.e)
ALL = ("dp", "seq")
NEG = -1e30
VMEM_LIMIT = 48 * 1024 * 1024


def product(a, b):
    return jnp.dot(a, b, preferred_element_type=F32)


def product_t(a, b):
    return lax.dot_general(a, b, (((1,), (1,)), ((), ())), preferred_element_type=F32)


def contract_rows(a, b):
    return lax.dot_general(a, b, (((0,), (0,)), ((), ())), preferred_element_type=F32)


def head_masks(rows):
    lane = lax.broadcasted_iota(jnp.int32, (rows, PAIR), 1)
    return (lane < HEAD, lane >= HEAD)


def only_head(value, h):
    mask = head_masks(value.shape[0])[h]
    return jnp.where(mask, value, jnp.zeros_like(value))


def block_kinds(qs_ref, ks_ref, i, j, qb, kb):
    q_first, q_last = qs_ref[i * qb], qs_ref[i * qb + qb - 1]
    k_first, k_last = ks_ref[j * kb], ks_ref[j * kb + kb - 1]
    live = jnp.logical_and(k_first <= q_last, k_last >= q_first)
    plain = jnp.logical_and(
        jnp.logical_and(q_first == q_last, k_first == k_last), q_first == k_first
    )
    return jnp.logical_and(live, jnp.logical_not(plain)), plain


def attend_kernel(qs_ref, ks_ref, q_ref, k_ref, v_ref, qid_ref, kid_ref, o_ref, lse_ref, vt_ref, m_ref, l_ref, acc_ref, *, kb):
    i = pl.program_id(1)
    qb = q_ref.shape[0]
    nk = k_ref.shape[0]
    scale = LOG2E / math.sqrt(HEAD)

    @pl.when(i == 0)
    def _():
        vt_ref[...] = v_ref[...].T

    m_ref[...] = jnp.full(m_ref.shape, NEG, F32)
    l_ref[...] = jnp.zeros(l_ref.shape, F32)
    acc_ref[...] = jnp.zeros(acc_ref.shape, F32)

    def step(j, masked):
        keys = k_ref[j * kb : (j + 1) * kb, :]
        if masked:
            allowed = kid_ref[j * kb : (j + 1) * kb, :] == qid_ref[...]
        for h in range(2):
            scores = product_t(keys, only_head(q_ref[...], h))
            if masked:
                scores = jnp.where(allowed, scores, NEG)
            m_old = m_ref[h : h + 1, :]
            m_new = jnp.maximum(m_old, jnp.max(scores, axis=0, keepdims=True))
            probs = jnp.exp2((scores - m_new) * scale)
            alpha = jnp.exp2((m_old - m_new) * scale)
            m_ref[h : h + 1, :] = m_new
            l_ref[h : h + 1, :] = l_ref[h : h + 1, :] * alpha + jnp.sum(probs, axis=0, keepdims=True)
            rows = slice(h * HEAD, (h + 1) * HEAD)
            acc_ref[rows, :] = acc_ref[rows, :] * alpha + product(
                vt_ref[rows, j * kb : (j + 1) * kb], probs.astype(BF)
            )

    for j in range(nk // kb):
        mixed, plain = block_kinds(qs_ref, ks_ref, i, j, qb, kb)
        pl.when(mixed)(lambda j=j: step(j, True))
        pl.when(plain)(lambda j=j: step(j, False))

    total = l_ref[0:2, :]
    lse_ref[0] = m_ref[0:2, :] * scale + jnp.log2(total)
    inverse = 1.0 / total
    out_t = jnp.concatenate(
        [acc_ref[0:HEAD, :] * inverse[0:1, :], acc_ref[HEAD:PAIR, :] * inverse[1:2, :]], axis=0
    )
    o_ref[...] = out_t.T.astype(BF)


def attend(q, k, v, offsets, heads, q_ids, k_ids):
    nq, nk = q.shape[0], k.shape[0]
    pairs = heads // 2
    qb, kb = min(256, nq), min(512, nk)
    q_off, k_off, v_off = offsets
    smem = pl.BlockSpec(memory_space=pltpu.SMEM)
    return pl.pallas_call(
        lambda *refs: attend_kernel(*refs, kb=kb),
        grid=(pairs, nq // qb),
        in_specs=[
            smem,
            smem,
            pl.BlockSpec((qb, PAIR), lambda p, i: (i, q_off + p)),
            pl.BlockSpec((nk, PAIR), lambda p, i: (0, k_off + p)),
            pl.BlockSpec((nk, PAIR), lambda p, i: (0, v_off + p)),
            pl.BlockSpec((1, qb), lambda p, i: (0, i)),
            pl.BlockSpec((nk, 1), lambda p, i: (0, 0)),
        ],
        out_specs=[
            pl.BlockSpec((qb, PAIR), lambda p, i: (i, p)),
            pl.BlockSpec((1, 2, qb), lambda p, i: (p, 0, i)),
        ],
        out_shape=[
            jax.ShapeDtypeStruct((nq, pairs * PAIR), BF),
            jax.ShapeDtypeStruct((pairs, 2, nq), F32),
        ],
        scratch_shapes=[
            pltpu.VMEM((PAIR, nk), BF),
            pltpu.VMEM((8, qb), F32),
            pltpu.VMEM((8, qb), F32),
            pltpu.VMEM((PAIR, qb), F32),
        ],
        compiler_params=pltpu.CompilerParams(vmem_limit_bytes=VMEM_LIMIT),
        cost_estimate=pl.CostEstimate(
            flops=8 * 2 * nq * nk * HEAD * heads, bytes_accessed=2 * heads * HEAD * (2 * nq + 2 * nk), transcendentals=nq * nk * heads
        ),
        name="attend",
    )(q_ids, k_ids, q, k, v, q_ids.reshape(1, nq), k_ids.reshape(nk, 1))


def attend_back_kernel(qs_ref, ks_ref, q_ref, k_ref, v_ref, do_ref, o_ref, lse_ref, qid_ref, kid_ref, dq_ref, dk_ref, dv_ref, kt_ref, dqt_ref, dk_acc, dv_acc, *, kb):
    i = pl.program_id(1)
    qb = q_ref.shape[0]
    nk = k_ref.shape[0]
    scale = LOG2E / math.sqrt(HEAD)

    @pl.when(i == 0)
    def _():
        kt_ref[...] = k_ref[...].T
        dk_acc[...] = jnp.zeros(dk_acc.shape, F32)
        dv_acc[...] = jnp.zeros(dv_acc.shape, F32)

    dqt_ref[...] = jnp.zeros(dqt_ref.shape, F32)
    both = (do_ref[...].astype(F32) * o_ref[...].astype(F32)).T
    deltas = (
        jnp.sum(both[0:HEAD, :], axis=0, keepdims=True),
        jnp.sum(both[HEAD:PAIR, :], axis=0, keepdims=True),
    )

    def step(j, masked):
        keys = k_ref[j * kb : (j + 1) * kb, :]
        values = v_ref[j * kb : (j + 1) * kb, :]
        if masked:
            allowed = kid_ref[j * kb : (j + 1) * kb, :] == qid_ref[...]
        for h in range(2):
            q_h = only_head(q_ref[...], h)
            do_h = only_head(do_ref[...], h)
            scores = product_t(keys, q_h)
            probs = jnp.exp2(scores * scale - lse_ref[0, h : h + 1, :])
            if masked:
                probs = jnp.where(allowed, probs, 0.0)
            grad_probs = product_t(values, do_h)
            grad_scores = (probs * (grad_probs - deltas[h])).astype(BF)
            dv_acc[j * kb : (j + 1) * kb, :] += product(probs.astype(BF), do_h)
            dk_acc[j * kb : (j + 1) * kb, :] += product(grad_scores, q_h)
            rows = slice(h * HEAD, (h + 1) * HEAD)
            dqt_ref[rows, :] += product(kt_ref[rows, j * kb : (j + 1) * kb], grad_scores)

    for j in range(nk // kb):
        mixed, plain = block_kinds(qs_ref, ks_ref, i, j, qb, kb)
        pl.when(mixed)(lambda j=j: step(j, True))
        pl.when(plain)(lambda j=j: step(j, False))

    dq_ref[...] = (dqt_ref[...] * (1.0 / math.sqrt(HEAD))).T.astype(BF)

    @pl.when(i == pl.num_programs(1) - 1)
    def _():
        dk_ref[...] = (dk_acc[...] * (1.0 / math.sqrt(HEAD))).astype(BF)
        dv_ref[...] = dv_acc[...].astype(BF)


def attend_back(q, k, v, offsets, heads, q_ids, k_ids, out, lse, grad_out):
    nq, nk = q.shape[0], k.shape[0]
    pairs = heads // 2
    qb, kb = min(256, nq), min(512, nk)
    q_off, k_off, v_off = offsets
    smem = pl.BlockSpec(memory_space=pltpu.SMEM)
    return pl.pallas_call(
        lambda *refs: attend_back_kernel(*refs, kb=kb),
        grid=(pairs, nq // qb),
        in_specs=[
            smem,
            smem,
            pl.BlockSpec((qb, PAIR), lambda p, i: (i, q_off + p)),
            pl.BlockSpec((nk, PAIR), lambda p, i: (0, k_off + p)),
            pl.BlockSpec((nk, PAIR), lambda p, i: (0, v_off + p)),
            pl.BlockSpec((qb, PAIR), lambda p, i: (i, p)),
            pl.BlockSpec((qb, PAIR), lambda p, i: (i, p)),
            pl.BlockSpec((1, 2, qb), lambda p, i: (p, 0, i)),
            pl.BlockSpec((1, qb), lambda p, i: (0, i)),
            pl.BlockSpec((nk, 1), lambda p, i: (0, 0)),
        ],
        out_specs=[
            pl.BlockSpec((qb, PAIR), lambda p, i: (i, p)),
            pl.BlockSpec((nk, PAIR), lambda p, i: (0, p)),
            pl.BlockSpec((nk, PAIR), lambda p, i: (0, p)),
        ],
        out_shape=[
            jax.ShapeDtypeStruct((nq, pairs * PAIR), BF),
            jax.ShapeDtypeStruct((nk, pairs * PAIR), BF),
            jax.ShapeDtypeStruct((nk, pairs * PAIR), BF),
        ],
        scratch_shapes=[
            pltpu.VMEM((PAIR, nk), BF),
            pltpu.VMEM((PAIR, qb), F32),
            pltpu.VMEM((nk, PAIR), F32),
            pltpu.VMEM((nk, PAIR), F32),
        ],
        compiler_params=pltpu.CompilerParams(vmem_limit_bytes=VMEM_LIMIT),
        cost_estimate=pl.CostEstimate(
            flops=20 * 2 * nq * nk * HEAD * heads, bytes_accessed=2 * heads * HEAD * (4 * nq + 4 * nk), transcendentals=nq * nk * heads
        ),
        name="attend_back",
    )(q_ids, k_ids, q, k, v, grad_out, out, lse, q_ids.reshape(1, nq), k_ids.reshape(nk, 1))


def bits_of(size):
    return [1 << b for b in range(size.bit_length() - 1)]


def swap(value, axis, bit, size):
    return lax.ppermute(value, axis, [(r, r ^ bit) for r in range(size)])


def my_bit(axis, bit):
    return (lax.axis_index(axis) // bit) % 2


def halve(value, axis_name, bit, size, where, last=False):
    mine = my_bit(axis_name, bit)
    keep = lax.dynamic_index_in_dim(value, mine, where, keepdims=False)
    send = lax.dynamic_index_in_dim(value, 1 - mine, where, keepdims=False)
    got = swap(send, axis_name, bit, size)
    total = keep.astype(F32) + got.astype(F32)
    return total if last else total.astype(value.dtype)


def scatter_dp(half, nd, dtype=BF):
    bits = bits_of(nd)[1:]
    cols = half.shape[-1]
    parts = []
    for part, order in enumerate((bits, bits[::-1])):
        piece = half[..., part * (cols // 2) : (part + 1) * (cols // 2)]
        piece = piece.reshape((2,) * len(bits) + piece.shape[1:])
        left = bits[::-1]
        for bit in order:
            where = left.index(bit)
            piece = halve(piece, "dp", bit, nd, where)
            left = [b for b in left if b != bit]
        parts.append(piece)
    return jnp.concatenate(parts, axis=-1)


def scatter_seq(rows, ns):
    bits = bits_of(ns)
    piece = rows.reshape((2,) * len(bits) + (rows.shape[0] // ns, rows.shape[1]))
    left = bits[::-1]
    for n, bit in enumerate(bits):
        where = left.index(bit)
        piece = halve(piece, "seq", bit, ns, where, last=n == len(bits) - 1)
        left = [b for b in left if b != bit]
    return piece


def core_half(x, grad, nd):
    rows = x.shape[1] // nd
    view = x.reshape(x.shape[0], nd // 2, 2, rows)
    mine = my_bit("dp", 1)
    x_keep = lax.dynamic_index_in_dim(view, mine, 2, keepdims=False).reshape(x.shape[0], -1)
    x_send = lax.dynamic_index_in_dim(view, 1 - mine, 2, keepdims=False).reshape(x.shape[0], -1)
    got = swap(contract_rows(x_send, grad).astype(BF), "dp", 1, nd)
    total = (contract_rows(x_keep, grad) + got.astype(F32)).astype(BF)
    return total.reshape(nd // 2, rows, grad.shape[1])


def weight_grad(x, grad, nd, ns):
    return scatter_seq(scatter_dp(core_half(x, grad, nd), nd), ns)


def norm_parts(values):
    centre = values - jnp.mean(values, axis=-1, keepdims=True)
    spread = jnp.mean(centre * centre, axis=-1, keepdims=True)
    inverse = lax.rsqrt(spread + 1e-05)
    return centre * inverse, inverse


def norm_back(unit, inverse, grad):
    return inverse * (
        grad
        - jnp.mean(grad, axis=-1, keepdims=True)
        - unit * jnp.mean(grad * unit, axis=-1, keepdims=True)
    )


def per_item(ids, rows):
    out = jnp.broadcast_to(rows[0:1, :], (ids.shape[0], rows.shape[1]))
    for n in range(1, rows.shape[0]):
        out = jnp.where(ids[:, None] == n, rows[n : n + 1, :], out)
    return out


def gelu_parts(pre):
    cdf = 0.5 * (1.0 + lax.erf(pre * (1.0 / math.sqrt(2.0))))
    density = jnp.exp(-0.5 * pre * pre) * (1.0 / math.sqrt(2.0 * math.pi))
    return (pre * cdf).astype(BF), (cdf + pre * density).astype(BF)


def block(nd, ns, tokens, patches, cameras, tri_items, patch_items, mod_weight, qkv_weight, self_out_weight, norm2_gain, norm2_bias, cross_q_weight, cross_kv_weight, cross_out_weight, norm3_gain, norm3_bias, mlp_in_weight, mlp_in_bias, mlp_out_weight, mlp_out_bias, cotangent):
    rows, width = tokens.shape
    ff = mlp_in_weight.shape[1]
    heads_here = HEADS // ns
    cols_here = width // ns
    seq = lax.axis_index("seq")

    def gather(w):
        return lax.all_gather(w, ALL, axis=0, tiled=True)

    token_all = lax.all_gather(tokens, "seq", axis=0, tiled=True)
    patch_all = lax.all_gather(patches, "seq", axis=0, tiled=True)
    qkv_mine = (
        qkv_weight.reshape(qkv_weight.shape[0], 3, ns, cols_here)
        .transpose(2, 0, 1, 3)
        .reshape(ns * qkv_weight.shape[0], 3 * cols_here)
    )
    qkv_mine = lax.all_to_all(qkv_mine, "seq", 0, 0, tiled=True)
    qkv_mine = lax.all_gather(qkv_mine, "dp", axis=0, tiled=True)

    small = jnp.concatenate(
        [
            mod_weight.reshape(-1),
            norm2_gain,
            norm2_bias,
            norm3_gain,
            norm3_bias,
            mlp_out_bias,
            mlp_in_bias,
        ]
    )
    small = lax.all_gather(small.reshape(1, -1), ALL, axis=0, tiled=True)
    mod_n = mod_weight.size
    own = norm2_gain.shape[0]
    mod_full = small[:, :mod_n].reshape(-1, mod_weight.shape[1])
    vectors = [small[:, mod_n + n * own : mod_n + (n + 1) * own].reshape(1, -1).astype(F32) for n in range(5)]
    gain_two, bias_two, gain_three, bias_three, out_bias = vectors
    in_bias = small[:, mod_n + 5 * own :].reshape(1, -1).astype(F32)

    w_self_out = gather(self_out_weight)
    w_cross_kv = gather(cross_kv_weight)
    w_cross_q = gather(cross_q_weight)
    w_cross_out = gather(cross_out_weight)
    w_in = gather(mlp_in_weight)
    w_out = gather(mlp_out_weight)

    my_items = lax.dynamic_slice_in_dim(tri_items, seq * rows, rows)

    mod_items = product_t(cameras, mod_full)
    unit_one, inv_one = norm_parts(token_all.astype(F32))
    act_one = (
        unit_one * (1.0 + per_item(tri_items, mod_items[:, width:])) + per_item(tri_items, mod_items[:, :width])
    ).astype(BF)
    qkv = product(act_one, qkv_mine).astype(BF)
    pairs_here = heads_here // 2
    self_off = (0, pairs_here, 2 * pairs_here)
    self_mine, self_lse = attend(qkv, qkv, qkv, self_off, heads_here, tri_items, tri_items)
    self_att = lax.all_to_all(self_mine, "seq", 0, 1, tiled=True)
    resid_in = tokens.astype(F32)
    resid_two = resid_in + product(self_att, w_self_out)

    unit_two, inv_two = norm_parts(resid_two)
    act_two = (unit_two * gain_two + bias_two).astype(BF)
    cross_q = product(act_two, w_cross_q).astype(BF)
    cross_kv = product(patch_all, w_cross_kv).astype(BF)
    cross_off = (0, 0, HEADS // 2)
    cross_att, cross_lse = attend(cross_q, cross_kv, cross_kv, cross_off, HEADS, my_items, patch_items)
    resid_three = resid_two + product(cross_att, w_cross_out)

    unit_three, inv_three = norm_parts(resid_three)
    act_three = (unit_three * gain_three + bias_three).astype(BF)
    pre = product(act_three, w_in) + in_bias
    hid, slope = gelu_parts(pre)
    block_out = (resid_three + product(hid, w_out) + out_bias).astype(BF)

    grad_out = cotangent.astype(F32)
    g_out_bias = jnp.sum(grad_out, axis=0)
    g_w_out = weight_grad(hid, cotangent, nd, ns)
    d_pre = (product_t(cotangent, w_out) * slope.astype(F32)).astype(BF)
    g_in_bias = jnp.sum(d_pre.astype(F32), axis=0)
    d_act_three = product_t(d_pre, w_in)
    g_w_in = weight_grad(act_three, d_pre, nd, ns)
    g_gain_three = jnp.sum(d_act_three * unit_three, axis=0)
    g_bias_three = jnp.sum(d_act_three, axis=0)
    d_resid_three = grad_out + norm_back(unit_three, inv_three, d_act_three * gain_three)

    d_cross_out = d_resid_three.astype(BF)
    d_cross = product_t(d_cross_out, w_cross_out).astype(BF)
    g_cross_out = weight_grad(cross_att, d_cross_out, nd, ns)
    d_cq, d_ck, d_cv = attend_back(
        cross_q, cross_kv, cross_kv, cross_off, HEADS, my_items, patch_items, cross_att, cross_lse, d_cross
    )
    d_ckv = jnp.concatenate([d_ck, d_cv], axis=1)
    d_act_two = product_t(d_cq, w_cross_q)
    g_gain_two = jnp.sum(d_act_two * unit_two, axis=0)
    g_bias_two = jnp.sum(d_act_two, axis=0)
    d_resid_two = d_resid_three + norm_back(unit_two, inv_two, d_act_two * gain_two)

    d_self_out = d_resid_two.astype(BF)
    d_self = product_t(d_self_out, w_self_out).astype(BF)
    d_self_mine = lax.all_to_all(d_self, "seq", 1, 0, tiled=True)
    g_cross_q = weight_grad(act_two, d_cq, nd, ns)
    g_cross_kv = weight_grad(patch_all, d_ckv, nd, ns)
    patch_grad = lax.psum_scatter(
        product_t(d_ckv, w_cross_kv).astype(BF), "seq", scatter_dimension=0, tiled=True
    ).astype(F32)
    g_self_out = weight_grad(self_att, d_self_out, nd, ns)
    d_q, d_k, d_v = attend_back(
        qkv, qkv, qkv, self_off, heads_here, tri_items, tri_items, self_mine, self_lse, d_self_mine
    )
    d_qkv = jnp.concatenate([d_q, d_k, d_v], axis=1)
    d_act_one_part = product_t(d_qkv, qkv_mine)

    shares = []
    for n in range(cameras.shape[0]):
        chosen = (tri_items == n)[:, None]
        shares.append(
            jnp.concatenate(
                [
                    jnp.sum(jnp.where(chosen, d_act_one_part, 0.0), axis=0),
                    jnp.sum(jnp.where(chosen, d_act_one_part * unit_one, 0.0), axis=0),
                ]
            )
        )
    g_mod_items = jnp.stack(shares)
    g_mod = lax.dot_general(
        g_mod_items, cameras.astype(F32), (((0,), (0,)), ((), ())), precision=lax.Precision.HIGHEST
    )

    d_act_one = lax.psum_scatter(d_act_one_part.astype(BF), "seq", scatter_dimension=0, tiled=True).astype(F32)
    g_qkv_dp = scatter_dp(core_half(act_one, d_qkv, nd), nd)
    g_qkv = lax.all_to_all(g_qkv_dp.astype(F32), "seq", 0, 0, tiled=True)
    g_qkv = (
        g_qkv.reshape(ns, qkv_weight.shape[0], 3, cols_here)
        .transpose(1, 2, 0, 3)
        .reshape(qkv_weight.shape)
    )
    unit_own, inv_own = norm_parts(resid_in)
    scale_own = per_item(my_items, mod_items[:, width:])
    input_grad = d_resid_two + norm_back(unit_own, inv_own, d_act_one * (1.0 + scale_own))

    def scatter_vector(value):
        return lax.psum_scatter(value, ALL, scatter_dimension=0, tiled=True)

    n_dev = nd * ns
    vector_grads = jnp.concatenate(
        [v.reshape(n_dev, -1) for v in (g_gain_two, g_bias_two, g_gain_three, g_bias_three, g_out_bias, g_in_bias)],
        axis=1,
    )
    vector_grads = scatter_vector(vector_grads.reshape(-1))
    g_mod = scatter_vector(g_mod)
    cut = [vector_grads[n * own : (n + 1) * own] for n in range(5)]
    return (
        block_out,
        input_grad,
        patch_grad,
        g_mod,
        g_qkv,
        g_self_out,
        cut[0],
        cut[1],
        g_cross_q,
        g_cross_kv,
        g_cross_out,
        cut[2],
        cut[3],
        g_w_in,
        vector_grads[5 * own :],
        g_w_out,
        cut[4],
    )


def solution(mesh):
    nd, ns = mesh.shape["dp"], mesh.shape["seq"]
    rows2, rows1 = P(ALL, None), P(ALL)
    placed = (rows2, rows2, P("dp", None), P("dp"), P("dp"), rows2, rows2, rows2, rows1, rows1, rows2, rows2, rows2, rows1, rows1, rows2, rows1, rows2, rows1, rows2)
    given = (rows2, rows2, rows2, rows2, rows2, rows2, rows1, rows1, rows2, rows2, rows2, rows1, rows1, rows2, rows1, rows2, rows1)

    def shards(*args):
        return block(nd, ns, *args)

    return jax.shard_map(shards, mesh=mesh, in_specs=placed, out_specs=given, check_vma=False)
```

```python
import functools
import math

import jax
import jax.numpy as jnp
from jax import lax
from jax.experimental import pallas as pl
from jax.experimental.pallas import tpu as pltpu
from jax.sharding import PartitionSpec as P

HEADS = 16
HEAD = 64
PAIR = 2 * HEAD
BF = jnp.bfloat16
F32 = jnp.float32
LOG2E = math.log2(math.e)
ALL = ("dp", "seq")
SOFT = LOG2E / math.sqrt(HEAD)
NEG = -1e30
VMEM_LIMIT = 56 * 1024 * 1024


def product(a, b):
    return jnp.dot(a, b, preferred_element_type=F32)


def product_t(a, b):
    return lax.dot_general(a, b, (((1,), (1,)), ((), ())), preferred_element_type=F32)


def contract_rows(a, b):
    return lax.dot_general(a, b, (((0,), (0,)), ((), ())), preferred_element_type=F32)


SHORT = pl.CostEstimate(flops=1, bytes_accessed=1, transcendentals=0)


def kernel_params():
    return pltpu.CompilerParams(vmem_limit_bytes=VMEM_LIMIT)


def head_lanes(rows, h):
    lane = lax.broadcasted_iota(jnp.int32, (rows, PAIR), 1)
    return (lane < HEAD, lane - HEAD) if h == 0 else (lane >= HEAD, lane)


def only_head(value, h):
    mine, _ = head_lanes(value.shape[0], h)
    return jnp.where(mine, value, jnp.zeros_like(value))


def tag_query(q, ids, h, items):
    mine, slot = head_lanes(q.shape[0], h)
    barred = jnp.where((slot != ids) & (slot >= 0) & (slot < items), NEG, 0.0)
    return jnp.where(mine, q.astype(F32), barred).astype(BF)


def tag_key(k, ids, h):
    mine, slot = head_lanes(k.shape[0], h)
    return jnp.where(mine, k.astype(F32), jnp.where(slot == ids, 1.0, 0.0)).astype(BF)


def with_ones(v, h):
    mine, _ = head_lanes(v.shape[0], h)
    return jnp.where(mine, v, jnp.ones_like(v))


def attend_kernel(q_ref, k_ref, v_ref, qid_ref, kid_ref, o_ref, lse_ref, key_ref, val_ref, *, items, heads):
    qb = q_ref.shape[0]

    @pl.when(pl.program_id(1) == 0)
    def _():
        for p in range(heads // 2):
            lanes = slice(p * PAIR, (p + 1) * PAIR)
            for h in range(2):
                key_ref[2 * p + h] = tag_key(k_ref[:, lanes], kid_ref[...], h)
                val_ref[2 * p + h] = with_ones(v_ref[:, lanes], h)

    for p in range(heads // 2):
        lanes = slice(p * PAIR, (p + 1) * PAIR)
        sums, tops = [], []
        for h in range(2):
            scores = product_t(tag_query(q_ref[:, lanes], qid_ref[...], h, items), key_ref[2 * p + h])
            top = jnp.max(scores, axis=1, keepdims=True)
            probs = jnp.exp2((scores - top) * SOFT).astype(BF)
            sums.append(product(probs, val_ref[2 * p + h]))
            tops.append(top)
        first = lax.broadcasted_iota(jnp.int32, (qb, PAIR), 1) < HEAD
        total = jnp.where(first, pltpu.roll(sums[0], HEAD, 1), pltpu.roll(sums[1], HEAD, 1))
        o_ref[:, lanes] = (jnp.where(first, sums[0], sums[1]) / total).astype(BF)
        lse = (jnp.where(first, tops[0], tops[1]) * SOFT + jnp.log2(total)).T
        lse_ref[p] = jnp.concatenate([lse[0:1], lse[HEAD : HEAD + 1]], axis=0)


def attend(q, k, v, starts, heads, q_ids, k_ids, items, first=0):
    nq, nk = q.shape[0], k.shape[0]
    step = min(4, heads)
    cols = step * HEAD
    qb = min(256, nq)
    q_off, k_off, v_off = (s // cols + first // step for s in starts)
    return pl.pallas_call(
        functools.partial(attend_kernel, items=items, heads=step),
        grid=(heads // step, nq // qb),
        in_specs=[
            pl.BlockSpec((qb, cols), lambda p, i: (i, q_off + p)),
            pl.BlockSpec((nk, cols), lambda p, i: (0, k_off + p)),
            pl.BlockSpec((nk, cols), lambda p, i: (0, v_off + p)),
            pl.BlockSpec((qb, 1), lambda p, i: (i, 0)),
            pl.BlockSpec((nk, 1), lambda p, i: (0, 0)),
        ],
        out_specs=[
            pl.BlockSpec((qb, cols), lambda p, i: (i, p)),
            pl.BlockSpec((step // 2, 2, qb), lambda p, i: (p, 0, i)),
        ],
        out_shape=[
            jax.ShapeDtypeStruct((nq, heads * HEAD), BF),
            jax.ShapeDtypeStruct((heads // 2, 2, nq), F32),
        ],
        scratch_shapes=[pltpu.VMEM((step, nk, PAIR), BF), pltpu.VMEM((step, nk, PAIR), BF)],
        compiler_params=kernel_params(),
        cost_estimate=SHORT,
        name="attend",
    )(q, k, v, q_ids, k_ids)


def attend_back_kernel(q_ref, k_ref, v_ref, do_ref, o_ref, lse_ref, qid_ref, kid_ref, dq_ref, dk_ref, dv_ref, key_ref, kt_ref, dk_sum, dv_sum, *, items, kb):
    i = pl.program_id(1)
    nk = k_ref.shape[0]

    @pl.when(i == 0)
    def _():
        kt_ref[...] = k_ref[...].T
        for h in range(2):
            key_ref[h] = tag_key(k_ref[...], kid_ref[...], h)
        dk_sum[...] = jnp.zeros(dk_sum.shape, F32)
        dv_sum[...] = jnp.zeros(dv_sum.shape, F32)

    q, do = q_ref[...], do_ref[...]
    both = (do.astype(F32) * o_ref[...].astype(F32)).T
    q_own = [only_head(q, h) for h in range(2)]
    do_own = [only_head(do, h) for h in range(2)]
    q_tag = [tag_query(q, qid_ref[...], h, items) for h in range(2)]
    delta = [jnp.sum(both[h * HEAD : (h + 1) * HEAD], axis=0, keepdims=True) for h in range(2)]
    dq = [None, None]
    for j in range(nk // kb):
        rows = slice(j * kb, (j + 1) * kb)
        probs_low, grads_low = [], []
        for h in range(2):
            scores = product_t(key_ref[h, rows, :], q_tag[h])
            probs = jnp.exp2(scores * SOFT - lse_ref[0, h : h + 1, :])
            grad_probs = product_t(v_ref[rows, :], do_own[h])
            grads_low.append((probs * (grad_probs - delta[h])).astype(BF))
            probs_low.append(probs.astype(BF))
            term = product(kt_ref[h * HEAD : (h + 1) * HEAD, rows], grads_low[h])
            dq[h] = term if dq[h] is None else dq[h] + term
        dv_sum[rows, :] += product(jnp.concatenate(probs_low, axis=1), jnp.concatenate(do_own, axis=0))
        dk_sum[rows, :] += product(jnp.concatenate(grads_low, axis=1), jnp.concatenate(q_own, axis=0))
    dq_ref[...] = (jnp.concatenate(dq, axis=0) * (1.0 / math.sqrt(HEAD))).T.astype(BF)

    @pl.when(i == pl.num_programs(1) - 1)
    def _():
        dk_ref[...] = (dk_sum[...] * (1.0 / math.sqrt(HEAD))).astype(BF)
        dv_ref[...] = dv_sum[...].astype(BF)


def attend_back(q, k, v, starts, heads, q_ids, k_ids, items, out, lse, grad_out, first=0):
    nq, nk = q.shape[0], k.shape[0]
    pairs = heads // 2
    qb, kb = min(512, nq), min(2048, nk)
    base = first // 2
    q_off, k_off, v_off = (s // PAIR + base for s in starts)
    mine = pl.BlockSpec((qb, PAIR), lambda p, i: (i, p + base))
    return pl.pallas_call(
        functools.partial(attend_back_kernel, items=items, kb=kb),
        grid=(pairs, nq // qb),
        in_specs=[
            pl.BlockSpec((qb, PAIR), lambda p, i: (i, q_off + p)),
            pl.BlockSpec((nk, PAIR), lambda p, i: (0, k_off + p)),
            pl.BlockSpec((nk, PAIR), lambda p, i: (0, v_off + p)),
            mine,
            mine,
            pl.BlockSpec((1, 2, qb), lambda p, i: (p + base, 0, i)),
            pl.BlockSpec((qb, 1), lambda p, i: (i, 0)),
            pl.BlockSpec((nk, 1), lambda p, i: (0, 0)),
        ],
        out_specs=[
            pl.BlockSpec((qb, PAIR), lambda p, i: (i, p)),
            pl.BlockSpec((nk, PAIR), lambda p, i: (0, p)),
            pl.BlockSpec((nk, PAIR), lambda p, i: (0, p)),
        ],
        out_shape=[
            jax.ShapeDtypeStruct((nq, pairs * PAIR), BF),
            jax.ShapeDtypeStruct((nk, pairs * PAIR), BF),
            jax.ShapeDtypeStruct((nk, pairs * PAIR), BF),
        ],
        scratch_shapes=[
            pltpu.VMEM((2, nk, PAIR), BF),
            pltpu.VMEM((PAIR, nk), BF),
            pltpu.VMEM((nk, PAIR), F32),
            pltpu.VMEM((nk, PAIR), F32),
        ],
        compiler_params=kernel_params(),
        cost_estimate=SHORT,
        name="attend_back",
    )(q, k, v, grad_out, out, lse, q_ids, k_ids)


def mlp_up_kernel(a_ref, w_ref, b_ref, hid_ref, slope_ref):
    pre = product(a_ref[...], w_ref[...]) + b_ref[...]
    cdf = 0.5 * (1.0 + lax.erf(pre * (1.0 / math.sqrt(2.0))))
    density = jnp.exp(-0.5 * pre * pre) * (1.0 / math.sqrt(2.0 * math.pi))
    hid_ref[...] = (pre * cdf).astype(BF)
    slope_ref[...] = (cdf + pre * density).astype(BF)


def mlp_up(act, w, bias):
    rows, ff = act.shape[0], w.shape[1]
    cb = 512
    block = pl.BlockSpec((rows, cb), lambda g: (0, g))
    return pl.pallas_call(
        mlp_up_kernel,
        grid=(ff // cb,),
        in_specs=[
            pl.BlockSpec(act.shape, lambda g: (0, 0)),
            pl.BlockSpec((w.shape[0], cb), lambda g: (0, g)),
            pl.BlockSpec((1, cb), lambda g: (0, g)),
        ],
        out_specs=[block, block],
        out_shape=[jax.ShapeDtypeStruct((rows, ff), BF)] * 2,
        compiler_params=kernel_params(),
        cost_estimate=SHORT,
        name="mlp_up",
    )(act, w, bias)


def mlp_back_kernel(g_ref, w_ref, slope_ref, out_ref, sum_ref):
    grad = product_t(g_ref[...], w_ref[...]) * slope_ref[...].astype(F32)
    low = grad.astype(BF)
    out_ref[...] = low
    sum_ref[...] = jnp.sum(low.astype(F32), axis=0, keepdims=True)


def mlp_back(grad, w, slope):
    rows, ff = slope.shape
    cb = 512
    block = pl.BlockSpec((rows, cb), lambda g: (0, g))
    return pl.pallas_call(
        mlp_back_kernel,
        grid=(ff // cb,),
        in_specs=[
            pl.BlockSpec(grad.shape, lambda g: (0, 0)),
            pl.BlockSpec((cb, w.shape[1]), lambda g: (g, 0)),
            block,
        ],
        out_specs=[block, pl.BlockSpec((1, cb), lambda g: (0, g))],
        out_shape=[jax.ShapeDtypeStruct((rows, ff), BF), jax.ShapeDtypeStruct((1, ff), F32)],
        compiler_params=kernel_params(),
        cost_estimate=SHORT,
        name="mlp_back",
    )(grad, w, slope)


def norm_parts(values):
    centre = values - jnp.mean(values, axis=-1, keepdims=True)
    spread = jnp.mean(centre * centre, axis=-1, keepdims=True)
    inverse = lax.rsqrt(spread + 1e-05)
    return centre * inverse, inverse


def norm_back(unit, inverse, grad):
    return inverse * (
        grad
        - jnp.mean(grad, axis=-1, keepdims=True)
        - unit * jnp.mean(grad * unit, axis=-1, keepdims=True)
    )


def per_item(ids, rows):
    out = jnp.broadcast_to(rows[0:1, :], (ids.shape[0], rows.shape[1]))
    for n in range(1, rows.shape[0]):
        out = jnp.where(ids == n, rows[n : n + 1, :], out)
    return out


def modulate_kernel(x_ref, id_ref, mod_ref, out_ref):
    width = x_ref.shape[1]
    unit, _ = norm_parts(x_ref[...].astype(F32))
    ids = id_ref[...]
    shift = per_item(ids, mod_ref[:, :width])
    scale = per_item(ids, mod_ref[:, width:])
    out_ref[...] = (unit * (1.0 + scale) + shift).astype(BF)


def modulate(x, ids, mod_items):
    rows, width = x.shape
    rb = 256
    return pl.pallas_call(
        modulate_kernel,
        grid=(rows // rb,),
        in_specs=[
            pl.BlockSpec((rb, width), lambda i: (i, 0)),
            pl.BlockSpec((rb, 1), lambda i: (i, 0)),
            pl.BlockSpec(mod_items.shape, lambda i: (0, 0)),
        ],
        out_specs=pl.BlockSpec((rb, width), lambda i: (i, 0)),
        out_shape=jax.ShapeDtypeStruct((rows, width), BF),
        compiler_params=kernel_params(),
        cost_estimate=SHORT,
        name="modulate",
    )(x, ids, mod_items)


def modulate_back_kernel(dq_ref, dk_ref, dv_ref, w_ref, x_ref, id_ref, out_ref, sum_ref):
    width = x_ref.shape[1]
    c = dq_ref.shape[1]
    items = sum_ref.shape[0]
    grad = product_t(dq_ref[...], w_ref[:, 0:c])
    grad += product_t(dk_ref[...], w_ref[:, c : 2 * c])
    grad += product_t(dv_ref[...], w_ref[:, 2 * c :])
    out_ref[...] = grad.astype(BF)

    @pl.when(pl.program_id(0) == 0)
    def _():
        sum_ref[...] = jnp.zeros(sum_ref.shape, F32)

    unit, _ = norm_parts(x_ref[...].astype(F32))
    times = grad * unit
    ids = id_ref[...]
    low, high = jnp.min(ids), jnp.max(ids)
    for n in range(items):
        @pl.when((low <= n) & (n <= high))
        def _():
            here = ids == n
            sum_ref[n : n + 1, :width] += jnp.sum(jnp.where(here, grad, 0.0), axis=0, keepdims=True)
            sum_ref[n : n + 1, width:] += jnp.sum(jnp.where(here, times, 0.0), axis=0, keepdims=True)


def modulate_back(d_q, d_k, d_v, w, x, ids, items):
    rows, width = x.shape
    rb = 256
    c = d_q.shape[1]
    part = pl.BlockSpec((rb, c), lambda i: (i, 0))
    return pl.pallas_call(
        modulate_back_kernel,
        grid=(rows // rb,),
        in_specs=[
            part,
            part,
            part,
            pl.BlockSpec(w.shape, lambda i: (0, 0)),
            pl.BlockSpec((rb, width), lambda i: (i, 0)),
            pl.BlockSpec((rb, 1), lambda i: (i, 0)),
        ],
        out_specs=[
            pl.BlockSpec((rb, width), lambda i: (i, 0)),
            pl.BlockSpec((items, 2 * width), lambda i: (0, 0)),
        ],
        out_shape=[jax.ShapeDtypeStruct((rows, width), BF), jax.ShapeDtypeStruct((items, 2 * width), F32)],
        compiler_params=kernel_params(),
        cost_estimate=SHORT,
        name="modulate_back",
    )(d_q, d_k, d_v, w, x, ids)


def grads_kernel(*refs, spans):
    n = len(spans)
    g = pl.program_id(0)
    x_refs, y_refs, out_ref, xt_ref = refs[:n], refs[n : 2 * n], refs[-2], refs[-1]
    for i, (start, stop) in enumerate(spans):
        rows = y_refs[i].shape[0]

        @pl.when(g == start)
        def _():
            xt_ref[:, :rows] = x_refs[i][...].T

        @pl.when((g >= start) & (g < stop))
        def _():
            out_ref[...] = product(xt_ref[:, :rows], y_refs[i][...]).astype(BF)


def weight_grads(pairs):
    width = pairs[0][0].shape[1]
    cb = min(1024, min(y.shape[1] for _, y in pairs))
    spans, at = [], 0
    for _, y in pairs:
        spans.append((at, at + y.shape[1] // cb))
        at = spans[-1][1]
    in_specs = [pl.BlockSpec(x.shape, lambda g: (0, 0), pipeline_mode=pl.Buffered(1)) for x, _ in pairs]
    for (_, y), (start, stop) in zip(pairs, spans):
        in_specs.append(
            pl.BlockSpec((y.shape[0], cb), lambda g, start=start, stop=stop: (0, jnp.clip(g - start, 0, stop - start - 1)))
        )
    longest = max(x.shape[0] for x, _ in pairs)
    return pl.pallas_call(
        functools.partial(grads_kernel, spans=tuple(spans)),
        grid=(at,),
        in_specs=in_specs,
        out_specs=pl.BlockSpec((width, cb), lambda g: (0, g)),
        scratch_shapes=[pltpu.VMEM((width, longest), BF)],
        out_shape=jax.ShapeDtypeStruct((width, at * cb), BF),
        compiler_params=kernel_params(),
        cost_estimate=SHORT,
        name="weight_grads",
    )(*[x for x, _ in pairs], *[y for _, y in pairs])


def bits_of(size):
    return [1 << b for b in range(size.bit_length() - 1)]


def swap(value, axis, bit, size):
    return lax.ppermute(value, axis, [(r, r ^ bit) for r in range(size)])


def my_bit(axis, bit):
    return (lax.axis_index(axis) // bit) % 2


def pick(value, index, where):
    return lax.dynamic_index_in_dim(value, index, where, keepdims=False)


def tie(first, rest):
    kept, rest = lax.optimization_barrier((first, rest))
    return kept, rest


def sum_xor(value, axis, size):
    me = lax.axis_index(axis)
    got = [swap(pick(value, me ^ m, 0), axis, m, size) for m in range(1, size)]
    return pick(value, me, 0), got


def add_all(own, got, dtype=F32):
    total = own.astype(F32)
    for value in got:
        total = total + value.astype(F32)
    return total.astype(dtype)


def gather_xor(value, axis, size):
    have = [value] + [swap(value, axis, m, size) for m in range(1, size)]
    return jnp.concatenate(natural(have, axis, size), axis=0)


def to_dp(whole):
    return lax.psum_scatter(whole, "dp", scatter_dimension=0, tiled=True)


def sync(*values):
    return lax.optimization_barrier(values)


def line_step(up, down, ns):
    return (
        lax.ppermute(up, "seq", [(r, r + 1) for r in range(ns - 1)]),
        lax.ppermute(down, "seq", [(r + 1, r) for r in range(ns - 1)]),
    )


def line_join(ups, downs, ns):
    turned = [ups[0]] + [downs[r] + ups[ns - r] for r in range(1, ns)]
    rows = ups[0].shape[0]
    twice = jnp.concatenate(turned + turned[:-1], axis=0)
    first = (ns - lax.axis_index("seq")) % ns
    return lax.dynamic_slice_in_dim(twice, first * rows, ns * rows)


class LineSum:
    def __init__(self, parts, ns):
        self.parts, self.ns, self.k = parts, ns, 0
        self.moved = None

    def chunk(self, d):
        rows = self.parts.shape[0] // self.ns
        return lax.dynamic_slice_in_dim(self.parts, jnp.clip(d, 0, self.ns - 1) * rows, rows).astype(F32)

    def start(self):
        self.k += 1
        k, ns, me = self.k, self.ns, lax.axis_index("seq")
        above, below = self.chunk(me + ns - k), self.chunk(me - ns + k)
        if self.moved is not None:
            above, below = above + self.moved[0].astype(F32), below + self.moved[1].astype(F32)
        self.moved = (
            lax.ppermute(above.astype(BF), "seq", [(r, r + 1) for r in range(k)]),
            lax.ppermute(below.astype(BF), "seq", [(ns - 1 - r, ns - 2 - r) for r in range(k)]),
        )

    def total(self):
        return self.chunk(lax.axis_index("seq")) + self.moved[0].astype(F32) + self.moved[1].astype(F32)


def natural(pieces, axis, size):
    pieces = list(pieces)
    for bit in bits_of(size):
        flip = my_bit(axis, bit) == 1
        out = list(pieces)
        for m in range(size):
            if not m & bit:
                out[m] = jnp.where(flip, pieces[m | bit], pieces[m])
                out[m | bit] = jnp.where(flip, pieces[m], pieces[m | bit])
        pieces = out
    return pieces


def exchange_start(blocks, ns):
    me = lax.axis_index("seq")
    return [pick(blocks, me, 0)] + [swap(pick(blocks, me ^ m, 0), "seq", m, ns) for m in range(1, ns)]


def join(pieces, axis, size):
    return jnp.concatenate(natural(pieces, axis, size), axis=0)


def xor_start(value, axis, size):
    return [value] + [swap(value, axis, m, size) for m in range(1, size)]


def double_start(have, bit, ns):
    return {**have, **{m | bit: swap(v, "seq", bit, ns) for m, v in have.items()}}


def block(nd, ns, tokens, patches, cameras, tri_items, patch_items, mod_weight, qkv_weight, self_out_weight, norm2_gain, norm2_bias, cross_q_weight, cross_kv_weight, cross_out_weight, norm3_gain, norm3_bias, mlp_in_weight, mlp_in_bias, mlp_out_weight, mlp_out_bias, cotangent):
    rows, width = tokens.shape
    heads_here = HEADS // ns
    cols_here = width // ns
    items = cameras.shape[0]
    seq = lax.axis_index("seq")

    seq_bits = bits_of(ns)[::-1]

    def over_dp(held):
        return lax.all_gather(join([held[m] for m in range(ns)], "seq", ns), "dp", axis=0, tiled=True)

    bundle = {0: jnp.concatenate([self_out_weight, cross_q_weight, cross_kv_weight, cross_out_weight], axis=1)}
    small = jnp.concatenate(
        [mod_weight.reshape(-1), norm2_gain, norm2_bias, norm3_gain, norm3_bias, mlp_out_bias, mlp_in_bias]
    )
    length = small.shape[0]
    small = jnp.pad(small, (0, -length % 2048)).reshape(-1, 128)
    qkv_cut = qkv_weight.reshape(qkv_weight.shape[0], 3, ns, cols_here).transpose(2, 0, 1, 3)
    qkv_cut = qkv_cut.reshape(ns, qkv_weight.shape[0], 3 * cols_here)

    ups, downs = [tokens], [tokens]
    qkv_mine = small_all = None
    todo = list(seq_bits)
    for k in range(1, ns):
        up, down = line_step(ups[-1], downs[-1], ns)
        if k == 1:
            small_got, qkv_got = xor_start(small, "seq", ns), exchange_start(qkv_cut, ns)
            bundle = double_start(bundle, todo.pop(0), ns)
            up, down, small_got, qkv_got, bundle = sync(up, down, small_got, qkv_got, bundle)
            qkv_mine = lax.all_gather(join(qkv_got, "seq", ns), "dp", axis=0, tiled=True)
        elif k == 2:
            small_got = xor_start(join(small_got, "seq", ns), "dp", nd)
            if todo:
                bundle = double_start(bundle, todo.pop(0), ns)
            up, down, small_got, bundle = sync(up, down, small_got, bundle)
            small_all = join(small_got, "dp", nd)
        else:
            up, down, small_all = sync(up, down, small_all)
        ups.append(up)
        downs.append(down)
    while todo:
        bundle = double_start(bundle, todo.pop(0), ns)
    if small_all is None:
        small_all = join(xor_start(join(small_got, "seq", ns), "dp", nd), "dp", nd)
    bundle = over_dp(bundle)
    small = small_all.reshape(nd * ns, -1)
    mod_n = mod_weight.size
    own = norm2_gain.shape[0]
    mod_full = small[:, :mod_n].reshape(-1, mod_weight.shape[1])
    vectors = [small[:, mod_n + n * own : mod_n + (n + 1) * own].reshape(1, -1).astype(F32) for n in range(5)]
    gain_two, bias_two, gain_three, bias_three, out_bias = vectors
    in_bias = small[:, mod_n + 5 * own : length].reshape(1, -1).astype(F32)

    tri_col, patch_col = tri_items.reshape(-1, 1), patch_items.reshape(-1, 1)
    my_col = lax.dynamic_slice_in_dim(tri_items, seq * rows, rows).reshape(-1, 1)

    mod_items = product_t(cameras, mod_full)
    token_all = line_join(ups, downs, ns)
    token_all, qkv_mine, patches, mlp_in_weight = sync(token_all, qkv_mine, patches, mlp_in_weight)
    patch_got = xor_start(patches, "seq", ns)
    act_one = modulate(token_all, tri_col, mod_items)
    w_in = double_start({0: mlp_in_weight}, seq_bits[0], ns)
    act_one, w_in = sync(act_one, w_in)
    for bit in seq_bits[1:]:
        w_in = double_start(w_in, bit, ns)
    qkv = product(act_one, qkv_mine).astype(BF)
    qkv, w_in, mlp_out_weight = sync(qkv, w_in, mlp_out_weight)
    w_in = over_dp(w_in)
    self_at = (0, cols_here, 2 * cols_here)
    self_mine, self_lse = attend(qkv, qkv, qkv, self_at, heads_here, tri_col, tri_col, items)
    self_mine, bundle, patch_got, mlp_out_weight = sync(self_mine, bundle, patch_got, mlp_out_weight)
    self_att = lax.all_to_all(self_mine, "seq", 0, 1, tiled=True)
    w_self_out = bundle[:, :width]
    w_cross_q = bundle[:, width : 2 * width]
    w_cross_kv = bundle[:, 2 * width : 4 * width]
    w_cross_out = bundle[:, 4 * width :]
    w_out = double_start({0: mlp_out_weight}, seq_bits[0], ns)
    patch_all = join(patch_got, "seq", ns)
    cross_kv = product(patch_all, w_cross_kv).astype(BF)
    self_att, cross_kv, w_out = sync(self_att, cross_kv, w_out)
    resid_in = tokens.astype(F32)
    resid_two = resid_in + product(self_att, w_self_out)

    unit_two, inv_two = norm_parts(resid_two)
    act_two = (unit_two * gain_two + bias_two).astype(BF)
    cross_q = product(act_two, w_cross_q).astype(BF)
    for bit in seq_bits[1:]:
        w_out = double_start(w_out, bit, ns)
    cross_q, w_out = sync(cross_q, w_out)
    w_out = over_dp(w_out)
    cross_at = (0, 0, width)
    cross_att, cross_lse = attend(cross_q, cross_kv, cross_kv, cross_at, HEADS, my_col, patch_col, items)
    resid_three = resid_two + product(cross_att, w_cross_out)

    unit_three, inv_three = norm_parts(resid_three)
    act_three = (unit_three * gain_three + bias_three).astype(BF)
    act_three, w_in = sync(act_three, w_in)
    hid, slope = mlp_up(act_three, w_in, in_bias)

    g_w_out = contract_rows(hid, cotangent).astype(BF)
    slope, g_w_out, w_out = sync(slope, g_w_out, w_out)
    g_w_out = to_dp(g_w_out)
    grad_out = cotangent.astype(F32)
    g_out_bias = jnp.sum(grad_out, axis=0)
    d_pre, g_in_bias = mlp_back(cotangent, w_out, slope)
    g_w_in = contract_rows(act_three, d_pre).astype(BF)
    d_pre, g_w_in = tie(d_pre, g_w_in)
    g_w_in = to_dp(g_w_in)
    d_act_three = product_t(d_pre, w_in)
    g_gain_three = jnp.sum(d_act_three * unit_three, axis=0)
    g_bias_three = jnp.sum(d_act_three, axis=0)
    d_resid_three = grad_out + norm_back(unit_three, inv_three, d_act_three * gain_three)

    d_cross_out = d_resid_three.astype(BF)
    d_cross = product_t(d_cross_out, w_cross_out).astype(BF)
    d_cq, d_ck, d_cv = attend_back(cross_q, cross_kv, cross_kv, cross_at, HEADS, my_col, patch_col, items, cross_att, cross_lse, d_cross)
    d_act_two = product_t(d_cq, w_cross_q)
    g_gain_two = jnp.sum(d_act_two * unit_two, axis=0)
    g_bias_two = jnp.sum(d_act_two, axis=0)
    d_resid_two = d_resid_three + norm_back(unit_two, inv_two, d_act_two * gain_two)

    d_self_out = d_resid_two.astype(BF)
    d_self = product_t(d_self_out, w_self_out).astype(BF)
    d_self_mine = lax.all_to_all(d_self, "seq", 1, 0, tiled=True)
    g_mid = weight_grads(
        [(self_att, d_self_out), (act_two, d_cq), (patch_all, d_ck), (patch_all, d_cv), (cross_att, d_cross_out)]
    )
    patch_part = (product_t(d_ck, w_cross_kv[:, :width]) + product_t(d_cv, w_cross_kv[:, width:])).astype(BF)
    block_out = (resid_three + product(hid, w_out) + out_bias).astype(BF)
    d_self_mine, g_mid, patch_part, block_out, g_w_out = sync(d_self_mine, g_mid, patch_part, block_out, g_w_out)

    def over_seq(value):
        return sum_xor(value.reshape((ns, -1) + value.shape[1:]), "seq", ns)

    g_mid = to_dp(g_mid)
    patch_sum, out_sum, in_sum = over_seq(patch_part), over_seq(g_w_out), None
    backs = []
    for first in range(0, heads_here, 2):
        back = attend_back(
            qkv, qkv, qkv, self_at, 2, tri_col, tri_col, items, self_mine, self_lse, d_self_mine, first=first
        )
        if in_sum is None:
            back, d_self_mine, g_w_in = sync(back, d_self_mine, g_w_in)
            in_sum = over_seq(g_w_in)
        backs.append(back)
    backs, patch_sum, out_sum = sync(backs, patch_sum, out_sum)
    d_q, d_k, d_v = (jnp.concatenate(p, axis=1) if len(p) > 1 else p[0] for p in zip(*backs))
    d_act_one_part, g_mod_items = modulate_back(d_q, d_k, d_v, qkv_mine, token_all, tri_col, items)
    d_act_one_part, g_mod_items, d_q, d_k, d_v, in_sum, patch_sum, out_sum = sync(
        d_act_one_part, g_mod_items, d_q, d_k, d_v, in_sum, patch_sum, out_sum
    )
    line = LineSum(d_act_one_part, ns)
    line.start()
    g_mod = lax.dot_general(
        g_mod_items, cameras.astype(F32), (((0,), (0,)), ((), ())), precision=lax.Precision.HIGHEST
    )
    n_dev = nd * ns
    tail = jnp.concatenate(
        [g_mod.reshape(n_dev, -1)]
        + [v.reshape(n_dev, -1) for v in (g_gain_two, g_bias_two, g_gain_three, g_bias_three, g_out_bias, g_in_bias)],
        axis=1,
    )
    tail_n = tail.shape[1]
    tail = jnp.pad(tail, ((0, 0), (0, -tail_n % 1024))).reshape(nd, ns, -1, 128)
    tail = sum_xor(tail, "dp", nd)
    g_qkv = weight_grads([(act_one, d_q), (act_one, d_k), (act_one, d_v)])
    g_qkv, line.moved, tail, patch_sum, out_sum, in_sum = sync(g_qkv, line.moved, tail, patch_sum, out_sum, in_sum)
    g_qkv = to_dp(g_qkv)
    for k in range(2, ns):
        line.start()
        if k == 2:
            tail = sum_xor(add_all(*tail), "seq", ns)
            patch_grad, g_w_out, g_w_in = add_all(*patch_sum), add_all(*out_sum), add_all(*in_sum)
            line.moved, tail, patch_grad, g_w_out, g_w_in, g_mid = sync(
                line.moved, tail, patch_grad, g_w_out, g_w_in, g_mid
            )
            g_mid = over_seq(g_mid)
            tail = add_all(*tail).reshape(-1)
    line.moved, g_mid, g_qkv = sync(line.moved, g_mid, g_qkv)
    d_act_one = line.total()
    g_mod = tail[:mod_n].reshape(mod_weight.shape)
    cut = [tail[mod_n + n * own : mod_n + (n + 1) * own] for n in range(5)]
    g_in_bias = tail[mod_n + 5 * own : tail_n]
    g_qkv = join(exchange_start(g_qkv.reshape(ns, -1, g_qkv.shape[1]), ns), "seq", ns).astype(F32)
    g_qkv = (
        g_qkv.reshape(ns, qkv_weight.shape[0], 3, cols_here)
        .transpose(1, 2, 0, 3)
        .reshape(qkv_weight.shape)
    )
    g_mid = add_all(*g_mid)
    unit_own, inv_own = norm_parts(resid_in)
    scale_own = per_item(my_col, mod_items[:, width:])
    input_grad = d_resid_two + norm_back(unit_own, inv_own, d_act_one * (1.0 + scale_own))
    return (
        block_out,
        input_grad,
        patch_grad,
        g_mod,
        g_qkv,
        g_mid[:, :width],
        cut[0],
        cut[1],
        g_mid[:, width : 2 * width],
        g_mid[:, 2 * width : 4 * width],
        g_mid[:, 4 * width :],
        cut[2],
        cut[3],
        g_w_in,
        g_in_bias,
        g_w_out,
        cut[4],
    )


def solution(mesh):
    nd, ns = mesh.shape["dp"], mesh.shape["seq"]
    rows2, rows1 = P(ALL, None), P(ALL)
    placed = (rows2, rows2, P("dp", None), P("dp"), P("dp"), rows2, rows2, rows2, rows1, rows1, rows2, rows2, rows2, rows1, rows1, rows2, rows1, rows2, rows1, rows2)
    given = (rows2, rows2, rows2, rows2, rows2, rows2, rows1, rows1, rows2, rows2, rows2, rows1, rows1, rows2, rows1, rows2, rows1)

    def shards(*args):
        return block(nd, ns, *args)

    return jax.shard_map(shards, mesh=mesh, in_specs=placed, out_specs=given, check_vma=False)
```

```python
import functools
import math

import jax
import jax.numpy as jnp
from jax import lax
from jax.experimental import pallas as pl
from jax.experimental.pallas import tpu as pltpu
from jax.sharding import PartitionSpec as P

HEADS = 16
HEAD = 64
PAIR = 2 * HEAD
BF = jnp.bfloat16
F32 = jnp.float32
LOG2E = math.log2(math.e)
ALL = ("dp", "seq")
SOFT = LOG2E / math.sqrt(HEAD)
NEG = -1e30
VMEM_LIMIT = 56 * 1024 * 1024


def product(a, b):
    return jnp.dot(a, b, preferred_element_type=F32)


def product_t(a, b):
    return lax.dot_general(a, b, (((1,), (1,)), ((), ())), preferred_element_type=F32)


def contract_rows(a, b):
    return lax.dot_general(a, b, (((0,), (0,)), ((), ())), preferred_element_type=F32)


SHORT = pl.CostEstimate(flops=1, bytes_accessed=1, transcendentals=0)


def kernel_params():
    return pltpu.CompilerParams(vmem_limit_bytes=VMEM_LIMIT)


def query_tags(ids, items):
    slot = lax.broadcasted_iota(jnp.int32, (ids.shape[0], PAIR), 1) % HEAD
    return jnp.where((slot != ids[:, None]) & (slot < items), NEG, 0.0).astype(BF)


def key_tags(ids):
    slot = lax.broadcasted_iota(jnp.int32, (ids.shape[0], PAIR), 1) % HEAD
    return jnp.where(slot == ids[:, None], 1.0, 0.0).astype(BF)


def in_head(value, h, other):
    lane = lax.broadcasted_iota(jnp.int32, value.shape, 1)
    return jnp.where((lane < HEAD) if h == 0 else (lane >= HEAD), value, other)


def only_head(value, h):
    return in_head(value, h, jnp.zeros_like(value))


def attend_kernel(q_ref, k_ref, v_ref, qtag_ref, ktag_ref, o_ref, lse_ref, key_ref, val_ref, *, heads):
    qb = q_ref.shape[0]

    @pl.when(pl.program_id(1) == 0)
    def _():
        for p in range(heads // 2):
            lanes = slice(p * PAIR, (p + 1) * PAIR)
            for h in range(2):
                key_ref[2 * p + h] = in_head(k_ref[:, lanes], h, ktag_ref[...])
                val_ref[2 * p + h] = in_head(v_ref[:, lanes], h, jnp.ones_like(ktag_ref))

    for p in range(heads // 2):
        lanes = slice(p * PAIR, (p + 1) * PAIR)
        sums, tops = [], []
        for h in range(2):
            scores = product_t(in_head(q_ref[:, lanes], h, qtag_ref[...]), key_ref[2 * p + h])
            top = jnp.max(scores, axis=1, keepdims=True)
            probs = jnp.exp2((scores - top) * SOFT).astype(BF)
            sums.append(product(probs, val_ref[2 * p + h]))
            tops.append(top)
        first = lax.broadcasted_iota(jnp.int32, (qb, PAIR), 1) < HEAD
        total = jnp.where(first, pltpu.roll(sums[0], HEAD, 1), pltpu.roll(sums[1], HEAD, 1))
        o_ref[:, lanes] = (jnp.where(first, sums[0], sums[1]) / total).astype(BF)
        lse = (jnp.where(first, tops[0], tops[1]) * SOFT + jnp.log2(total)).T
        lse_ref[p] = jnp.concatenate([lse[0:1], lse[HEAD : HEAD + 1]], axis=0)


def attend(q, k, v, starts, heads, q_tags, k_tags):
    nq, nk = q.shape[0], k.shape[0]
    step = min(4, heads)
    cols = step * HEAD
    qb = min(256 * max(1, 2048 // nk), nq)
    q_off, k_off, v_off = (s // cols for s in starts)
    return pl.pallas_call(
        functools.partial(attend_kernel, heads=step),
        grid=(heads // step, nq // qb),
        in_specs=[
            pl.BlockSpec((qb, cols), lambda p, i: (i, q_off + p)),
            pl.BlockSpec((nk, cols), lambda p, i: (0, k_off + p)),
            pl.BlockSpec((nk, cols), lambda p, i: (0, v_off + p)),
            pl.BlockSpec((qb, PAIR), lambda p, i: (i, 0)),
            pl.BlockSpec((nk, PAIR), lambda p, i: (0, 0)),
        ],
        out_specs=[
            pl.BlockSpec((qb, cols), lambda p, i: (i, p)),
            pl.BlockSpec((step // 2, 2, qb), lambda p, i: (p, 0, i)),
        ],
        out_shape=[
            jax.ShapeDtypeStruct((nq, heads * HEAD), BF),
            jax.ShapeDtypeStruct((heads // 2, 2, nq), F32),
        ],
        scratch_shapes=[pltpu.VMEM((step, nk, PAIR), BF), pltpu.VMEM((step, nk, PAIR), BF)],
        compiler_params=kernel_params(),
        cost_estimate=SHORT,
        name="attend",
    )(q, k, v, q_tags, k_tags)


def attend_back_kernel(q_ref, k_ref, v_ref, do_ref, o_ref, lse_ref, qtag_ref, ktag_ref, dq_ref, dk_ref, dv_ref, key_ref, kt_ref, dk_sum, dv_sum, *, kb):
    i = pl.program_id(1)
    nk = k_ref.shape[0]

    @pl.when(i == 0)
    def _():
        kt_ref[...] = k_ref[...].T
        for h in range(2):
            key_ref[h] = in_head(k_ref[...], h, ktag_ref[...])
        dk_sum[...] = jnp.zeros(dk_sum.shape, F32)
        dv_sum[...] = jnp.zeros(dv_sum.shape, F32)

    q, do = q_ref[...], do_ref[...]
    both = (do.astype(F32) * o_ref[...].astype(F32)).T
    q_own = [only_head(q, h) for h in range(2)]
    do_own = [only_head(do, h) for h in range(2)]
    q_tag = [in_head(q, h, qtag_ref[...]) for h in range(2)]
    delta = [jnp.sum(both[h * HEAD : (h + 1) * HEAD], axis=0, keepdims=True) for h in range(2)]
    dq = [None, None]
    for j in range(nk // kb):
        rows = slice(j * kb, (j + 1) * kb)
        probs_low, grads_low = [], []
        for h in range(2):
            scores = product_t(key_ref[h, rows, :], q_tag[h])
            probs = jnp.exp2(scores * SOFT - lse_ref[0, h : h + 1, :])
            grad_probs = product_t(v_ref[rows, :], do_own[h])
            grads_low.append((probs * (grad_probs - delta[h])).astype(BF))
            probs_low.append(probs.astype(BF))
            term = product(kt_ref[h * HEAD : (h + 1) * HEAD, rows], grads_low[h])
            dq[h] = term if dq[h] is None else dq[h] + term
        dv_sum[rows, :] += product(jnp.concatenate(probs_low, axis=1), jnp.concatenate(do_own, axis=0))
        dk_sum[rows, :] += product(jnp.concatenate(grads_low, axis=1), jnp.concatenate(q_own, axis=0))
    dq_ref[...] = (jnp.concatenate(dq, axis=0) * (1.0 / math.sqrt(HEAD))).T.astype(BF)

    @pl.when(i == pl.num_programs(1) - 1)
    def _():
        dk_ref[...] = (dk_sum[...] * (1.0 / math.sqrt(HEAD))).astype(BF)
        dv_ref[...] = dv_sum[...].astype(BF)


def attend_back(q, k, v, starts, heads, q_tags, k_tags, out, lse, grad_out, first=0):
    nq, nk = q.shape[0], k.shape[0]
    pairs = heads // 2
    qb, kb = min(512, nq), min(2048, nk)
    base = first // 2
    q_off, k_off, v_off = (s // PAIR + base for s in starts)
    mine = pl.BlockSpec((qb, PAIR), lambda p, i: (i, p + base))
    return pl.pallas_call(
        functools.partial(attend_back_kernel, kb=kb),
        grid=(pairs, nq // qb),
        in_specs=[
            pl.BlockSpec((qb, PAIR), lambda p, i: (i, q_off + p)),
            pl.BlockSpec((nk, PAIR), lambda p, i: (0, k_off + p)),
            pl.BlockSpec((nk, PAIR), lambda p, i: (0, v_off + p)),
            mine,
            mine,
            pl.BlockSpec((1, 2, qb), lambda p, i: (p + base, 0, i)),
            pl.BlockSpec((qb, PAIR), lambda p, i: (i, 0)),
            pl.BlockSpec((nk, PAIR), lambda p, i: (0, 0)),
        ],
        out_specs=[
            pl.BlockSpec((qb, PAIR), lambda p, i: (i, p)),
            pl.BlockSpec((nk, PAIR), lambda p, i: (0, p)),
            pl.BlockSpec((nk, PAIR), lambda p, i: (0, p)),
        ],
        out_shape=[
            jax.ShapeDtypeStruct((nq, pairs * PAIR), BF),
            jax.ShapeDtypeStruct((nk, pairs * PAIR), BF),
            jax.ShapeDtypeStruct((nk, pairs * PAIR), BF),
        ],
        scratch_shapes=[
            pltpu.VMEM((2, nk, PAIR), BF),
            pltpu.VMEM((PAIR, nk), BF),
            pltpu.VMEM((nk, PAIR), F32),
            pltpu.VMEM((nk, PAIR), F32),
        ],
        compiler_params=kernel_params(),
        cost_estimate=SHORT,
        name="attend_back",
    )(q, k, v, grad_out, out, lse, q_tags, k_tags)


def mlp_up_kernel(a_ref, w_ref, b_ref, hid_ref, slope_ref):
    pre = product(a_ref[...], w_ref[...]) + b_ref[...]
    cdf = 0.5 * (1.0 + lax.erf(pre * (1.0 / math.sqrt(2.0))))
    density = jnp.exp(-0.5 * pre * pre) * (1.0 / math.sqrt(2.0 * math.pi))
    hid_ref[...] = (pre * cdf).astype(BF)
    slope_ref[...] = (cdf + pre * density).astype(BF)


def mlp_up(act, w, bias):
    rows, ff = act.shape[0], w.shape[1]
    cb = 512
    block = pl.BlockSpec((rows, cb), lambda g: (0, g))
    return pl.pallas_call(
        mlp_up_kernel,
        grid=(ff // cb,),
        in_specs=[
            pl.BlockSpec(act.shape, lambda g: (0, 0)),
            pl.BlockSpec((w.shape[0], cb), lambda g: (0, g)),
            pl.BlockSpec((1, cb), lambda g: (0, g)),
        ],
        out_specs=[block, block],
        out_shape=[jax.ShapeDtypeStruct((rows, ff), BF)] * 2,
        compiler_params=kernel_params(),
        cost_estimate=SHORT,
        name="mlp_up",
    )(act, w, bias)


def mlp_back_kernel(g_ref, w_ref, slope_ref, out_ref, sum_ref):
    grad = product_t(g_ref[...], w_ref[...]) * slope_ref[...].astype(F32)
    low = grad.astype(BF)
    out_ref[...] = low
    sum_ref[...] = jnp.sum(low.astype(F32), axis=0, keepdims=True)


def mlp_back(grad, w, slope):
    rows, ff = slope.shape
    cb = 512
    block = pl.BlockSpec((rows, cb), lambda g: (0, g))
    return pl.pallas_call(
        mlp_back_kernel,
        grid=(ff // cb,),
        in_specs=[
            pl.BlockSpec(grad.shape, lambda g: (0, 0)),
            pl.BlockSpec((cb, w.shape[1]), lambda g: (g, 0)),
            block,
        ],
        out_specs=[block, pl.BlockSpec((1, cb), lambda g: (0, g))],
        out_shape=[jax.ShapeDtypeStruct((rows, ff), BF), jax.ShapeDtypeStruct((1, ff), F32)],
        compiler_params=kernel_params(),
        cost_estimate=SHORT,
        name="mlp_back",
    )(grad, w, slope)


def norm_parts(values):
    centre = values - jnp.mean(values, axis=-1, keepdims=True)
    spread = jnp.mean(centre * centre, axis=-1, keepdims=True)
    inverse = lax.rsqrt(spread + 1e-05)
    return centre * inverse, inverse


def norm_back(unit, inverse, grad):
    return inverse * (
        grad
        - jnp.mean(grad, axis=-1, keepdims=True)
        - unit * jnp.mean(grad * unit, axis=-1, keepdims=True)
    )


def per_item(ids, rows):
    out = jnp.broadcast_to(rows[0:1, :], (ids.shape[0], rows.shape[1]))
    for n in range(1, rows.shape[0]):
        out = jnp.where(ids == n, rows[n : n + 1, :], out)
    return out


def modulate_kernel(me_ref, *refs, per, offsets):
    pieces, (id_ref, mod_ref, out_ref, x_ref) = refs[:-4], refs[-4:]
    width = out_ref.shape[1]
    block = pl.program_id(0) // per
    for off, piece in zip(offsets, pieces):
        @pl.when(me_ref[0] + off == block)
        def _():
            x_ref[...] = piece[...]

    unit, _ = norm_parts(x_ref[...].astype(F32))
    ids = id_ref[...]
    shift = per_item(ids, mod_ref[:, :width])
    scale = per_item(ids, mod_ref[:, width:])
    out_ref[...] = (unit * (1.0 + scale) + shift).astype(BF)


def modulate(pieces, offsets, me, ids, mod_items):
    rows, width = pieces[0].shape
    rb = min(256, rows)
    per = rows // rb
    total = ids.shape[0]
    block = pl.BlockSpec((rb, width), lambda i, me: (i, 0))
    return pl.pallas_call(
        functools.partial(modulate_kernel, per=per, offsets=offsets),
        grid_spec=pltpu.PrefetchScalarGridSpec(
            num_scalar_prefetch=1,
            grid=(total // rb,),
            in_specs=[
                pl.BlockSpec((rb, width), lambda i, me, off=off: (jnp.where(me[0] + off == i // per, i % per, 0), 0))
                for off in offsets
            ]
            + [
                pl.BlockSpec((rb, 1), lambda i, me: (i, 0)),
                pl.BlockSpec(mod_items.shape, lambda i, me: (0, 0)),
            ],
            out_specs=[block, block],
        ),
        out_shape=[jax.ShapeDtypeStruct((total, width), BF)] * 2,
        compiler_params=kernel_params(),
        cost_estimate=SHORT,
        name="modulate",
    )(me.reshape(1), *pieces, ids, mod_items)


def modulate_back_kernel(dq_ref, dk_ref, dv_ref, w_ref, x_ref, id_ref, out_ref, sum_ref):
    width = x_ref.shape[1]
    c = dq_ref.shape[1]
    items = sum_ref.shape[0]
    grad = product_t(dq_ref[...], w_ref[:, 0:c])
    grad += product_t(dk_ref[...], w_ref[:, c : 2 * c])
    grad += product_t(dv_ref[...], w_ref[:, 2 * c :])
    out_ref[...] = grad.astype(BF)

    @pl.when(pl.program_id(0) == 0)
    def _():
        sum_ref[...] = jnp.zeros(sum_ref.shape, F32)

    unit, _ = norm_parts(x_ref[...].astype(F32))
    times = grad * unit
    ids = id_ref[...]
    low, high = jnp.min(ids), jnp.max(ids)
    for n in range(items):
        @pl.when((low <= n) & (n <= high))
        def _():
            here = ids == n
            sum_ref[n : n + 1, :width] += jnp.sum(jnp.where(here, grad, 0.0), axis=0, keepdims=True)
            sum_ref[n : n + 1, width:] += jnp.sum(jnp.where(here, times, 0.0), axis=0, keepdims=True)


def modulate_back(d_q, d_k, d_v, w, x, ids, items):
    rows, width = x.shape
    rb = 256
    c = d_q.shape[1]
    part = pl.BlockSpec((rb, c), lambda i: (i, 0))
    return pl.pallas_call(
        modulate_back_kernel,
        grid=(rows // rb,),
        in_specs=[
            part,
            part,
            part,
            pl.BlockSpec(w.shape, lambda i: (0, 0)),
            pl.BlockSpec((rb, width), lambda i: (i, 0)),
            pl.BlockSpec((rb, 1), lambda i: (i, 0)),
        ],
        out_specs=[
            pl.BlockSpec((rb, width), lambda i: (i, 0)),
            pl.BlockSpec((items, 2 * width), lambda i: (0, 0)),
        ],
        out_shape=[jax.ShapeDtypeStruct((rows, width), BF), jax.ShapeDtypeStruct((items, 2 * width), F32)],
        compiler_params=kernel_params(),
        cost_estimate=SHORT,
        name="modulate_back",
    )(d_q, d_k, d_v, w, x, ids)


def grads_kernel(*refs, spans):
    n = len(spans)
    g = pl.program_id(0)
    x_refs, y_refs, out_ref, xt_ref = refs[:n], refs[n : 2 * n], refs[-2], refs[-1]
    for i, (start, stop) in enumerate(spans):
        rows = y_refs[i].shape[0]

        @pl.when(g == start)
        def _():
            xt_ref[:, :rows] = x_refs[i][...].T

        @pl.when((g >= start) & (g < stop))
        def _():
            out_ref[...] = product(xt_ref[:, :rows], y_refs[i][...]).astype(BF)


def weight_grads(pairs):
    width = pairs[0][0].shape[1]
    cb = min(1024, min(y.shape[1] for _, y in pairs))
    spans, at = [], 0
    for _, y in pairs:
        spans.append((at, at + y.shape[1] // cb))
        at = spans[-1][1]
    in_specs = [pl.BlockSpec(x.shape, lambda g: (0, 0), pipeline_mode=pl.Buffered(1)) for x, _ in pairs]
    for (_, y), (start, stop) in zip(pairs, spans):
        in_specs.append(
            pl.BlockSpec((y.shape[0], cb), lambda g, start=start, stop=stop: (0, jnp.clip(g - start, 0, stop - start - 1)))
        )
    longest = max(x.shape[0] for x, _ in pairs)
    return pl.pallas_call(
        functools.partial(grads_kernel, spans=tuple(spans)),
        grid=(at,),
        in_specs=in_specs,
        out_specs=pl.BlockSpec((width, cb), lambda g: (0, g)),
        scratch_shapes=[pltpu.VMEM((width, longest), BF)],
        out_shape=jax.ShapeDtypeStruct((width, at * cb), BF),
        compiler_params=kernel_params(),
        cost_estimate=SHORT,
        name="weight_grads",
    )(*[x for x, _ in pairs], *[y for _, y in pairs])


def bits_of(size):
    return [1 << b for b in range(size.bit_length() - 1)]


class Axis:
    def __init__(self, name, length, size, me, flip):
        self.name, self.length, self.size, self.me, self.flip = name, length, size, me, flip

    def send(self, value, m):
        return lax.ppermute(value, self.name, [(r, r ^ self.flip(m)) for r in range(self.length)])

    def mine(self, bit):
        return (self.me // bit) % 2


def pick(value, index, where):
    return lax.dynamic_index_in_dim(value, index, where, keepdims=False)


def sync(*values):
    return lax.optimization_barrier(values)


def natural(pieces, axis):
    pieces = list(pieces)
    for bit in bits_of(axis.size):
        flip = axis.mine(bit) == 1
        out = list(pieces)
        for m in range(axis.size):
            if not m & bit:
                out[m] = jnp.where(flip, pieces[m | bit], pieces[m])
                out[m | bit] = jnp.where(flip, pieces[m], pieces[m | bit])
        pieces = out
    return pieces


def join(pieces, axis):
    if isinstance(pieces, dict):
        pieces = [pieces[m] for m in range(axis.size)]
    return jnp.concatenate(natural(pieces, axis), axis=0)


def exchange_start(blocks, axis):
    return [pick(blocks, axis.me ^ m, 0) if m == 0 else axis.send(pick(blocks, axis.me ^ m, 0), m) for m in range(axis.size)]


def xor_start(value, axis):
    return [value] + [axis.send(value, m) for m in range(1, axis.size)]


def double_start(have, bit, axis):
    return {**have, **{m | bit: axis.send(v, bit) for m, v in have.items()}}


class LineSum:
    def __init__(self, parts, ns):
        self.parts, self.ns, self.k = parts, ns, 0
        self.moved = None

    def chunk(self, d):
        rows = self.parts.shape[0] // self.ns
        return lax.dynamic_slice_in_dim(self.parts, jnp.clip(d, 0, self.ns - 1) * rows, rows).astype(F32)

    def start(self):
        self.k += 1
        k, ns, me = self.k, self.ns, lax.axis_index("seq")
        above, below = self.chunk(me + ns - k), self.chunk(me - ns + k)
        if self.moved is not None:
            above, below = above + self.moved[0].astype(F32), below + self.moved[1].astype(F32)
        self.moved = (
            lax.ppermute(above.astype(BF), "seq", [(r, r + 1) for r in range(k)]),
            lax.ppermute(below.astype(BF), "seq", [(ns - 1 - r, ns - 2 - r) for r in range(k)]),
        )

    def total(self):
        return self.chunk(lax.axis_index("seq")) + self.moved[0].astype(F32) + self.moved[1].astype(F32)


def line_step(up, down, ns):
    return (
        lax.ppermute(up, "seq", [(r, r + 1) for r in range(ns - 1)]),
        lax.ppermute(down, "seq", [(r + 1, r) for r in range(ns - 1)]),
    )


def add_all(pieces, dtype=F32):
    total = pieces[0].astype(F32)
    for value in pieces[1:]:
        total = total + value.astype(F32)
    return total.astype(dtype)


def to_dp(whole):
    return lax.psum_scatter(whole, "dp", scatter_dimension=0, tiled=True)


def block(nd, ns, tokens, patches, cameras, tri_items, patch_items, mod_weight, qkv_weight, self_out_weight, norm2_gain, norm2_bias, cross_q_weight, cross_kv_weight, cross_out_weight, norm3_gain, norm3_bias, mlp_in_weight, mlp_in_bias, mlp_out_weight, mlp_out_bias, cotangent):
    rows, width = tokens.shape
    heads_here = HEADS // ns
    cols_here = width // ns
    items = cameras.shape[0]
    w_rows = qkv_weight.shape[0]
    n_dev = nd * ns
    seq = Axis("seq", ns, ns, lax.axis_index("seq"), lambda m: m)

    def over_dp(held):
        return lax.all_gather(join(held, seq), "dp", axis=0, tiled=True)

    down_bits = bits_of(ns)[::-1]

    bundle = {0: jnp.concatenate([self_out_weight, cross_q_weight, cross_kv_weight, cross_out_weight], axis=1)}
    small = jnp.concatenate(
        [mod_weight.reshape(-1), norm2_gain, norm2_bias, norm3_gain, norm3_bias, mlp_out_bias, mlp_in_bias]
    )
    length = small.shape[0]
    extra = -(-length // w_rows)
    extra += -extra % 128
    small = jnp.pad(small, (0, extra * w_rows - length)).reshape(w_rows, extra)
    cut = qkv_weight.reshape(w_rows, 3, ns, cols_here).transpose(2, 0, 1, 3).reshape(ns, w_rows, 3 * cols_here)
    cut = jnp.concatenate([cut, jnp.broadcast_to(small[None], (ns, w_rows, extra))], axis=2)

    ups, downs = [tokens], [tokens]
    todo = list(down_bits)
    for k in range(1, ns):
        up, down = line_step(ups[-1], downs[-1], ns)
        if k == 1:
            cut = exchange_start(cut, seq)
            up, down, cut = sync(up, down, cut)
            cut = lax.all_gather(join(cut, seq), "dp", axis=0, tiled=True)
        else:
            if todo:
                bundle = double_start(bundle, todo.pop(0), seq)
            up, down, bundle = sync(up, down, bundle)
        ups.append(up)
        downs.append(down)
    while todo:
        bundle = double_start(bundle, todo.pop(0), seq)
    ups, downs, cut, patches, mlp_in_weight = sync(ups, downs, cut, patches, mlp_in_weight)
    qkv_mine = cut[:, : 3 * cols_here]
    small = cut[:, 3 * cols_here :].reshape(n_dev, -1)
    bundle = over_dp(bundle)
    mod_n = mod_weight.size
    own = norm2_gain.shape[0]
    mod_full = small[:, :mod_n].reshape(-1, mod_weight.shape[1])
    vectors = [small[:, mod_n + n * own : mod_n + (n + 1) * own].reshape(1, -1).astype(F32) for n in range(5)]
    gain_two, bias_two, gain_three, bias_three, out_bias = vectors
    in_bias = small[:, mod_n + 5 * own : length].reshape(1, -1).astype(F32)

    tri_col = tri_items.reshape(-1, 1)
    tri_query, tri_key = query_tags(tri_items, items), key_tags(tri_items)
    my_items = lax.dynamic_slice_in_dim(tri_items, seq.me * rows, rows)
    my_query, patch_key = query_tags(my_items, items), key_tags(patch_items)

    mod_items = product_t(cameras, mod_full)
    patch_all = xor_start(patches, seq)
    w_in = double_start({0: mlp_in_weight}, down_bits[0], seq)
    steps = range(1, ns)
    act_one, token_all = modulate(
        [tokens] + ups[1:] + downs[1:], [0] + [-k for k in steps] + list(steps), seq.me, tri_col, mod_items
    )
    act_one, w_in = sync(act_one, w_in)
    for bit in down_bits[1:]:
        w_in = double_start(w_in, bit, seq)
    qkv = product(act_one, qkv_mine).astype(BF)
    qkv, w_in, mlp_out_weight = sync(qkv, w_in, mlp_out_weight)
    w_in = over_dp(w_in)
    w_out = double_start({0: mlp_out_weight}, down_bits[0], seq)
    self_at = (0, cols_here, 2 * cols_here)
    self_mine, self_lse = attend(qkv, qkv, qkv, self_at, heads_here, tri_query, tri_key)
    self_mine, bundle, patch_all, w_out = sync(self_mine, bundle, patch_all, w_out)
    w_self_out = bundle[:, :width]
    w_cross_q = bundle[:, width : 2 * width]
    w_cross_kv = bundle[:, 2 * width : 4 * width]
    w_cross_out = bundle[:, 4 * width :]
    self_att = lax.all_to_all(self_mine, "seq", 0, 1, tiled=True)
    patch_all = join(patch_all, seq)
    cross_kv = product(patch_all, w_cross_kv).astype(BF)
    self_att, cross_kv = sync(self_att, cross_kv)
    for bit in down_bits[1:]:
        w_out = double_start(w_out, bit, seq)
    resid_in = tokens.astype(F32)
    resid_two = resid_in + product(self_att, w_self_out)

    unit_two, inv_two = norm_parts(resid_two)
    act_two = (unit_two * gain_two + bias_two).astype(BF)
    cross_q = product(act_two, w_cross_q).astype(BF)
    cross_q, w_out = sync(cross_q, w_out)
    w_out = over_dp(w_out)
    cross_at = (0, 0, width)
    cross_att, cross_lse = attend(cross_q, cross_kv, cross_kv, cross_at, HEADS, my_query, patch_key)
    resid_three = resid_two + product(cross_att, w_cross_out)

    unit_three, inv_three = norm_parts(resid_three)
    act_three = (unit_three * gain_three + bias_three).astype(BF)
    act_three, w_in = sync(act_three, w_in)
    hid, slope = mlp_up(act_three, w_in, in_bias)

    g_w_out = contract_rows(hid, cotangent).astype(BF)
    slope, g_w_out, w_out = sync(slope, g_w_out, w_out)
    g_w_out = to_dp(g_w_out)
    grad_out = cotangent.astype(F32)
    g_out_bias = jnp.sum(grad_out, axis=0)
    d_pre, g_in_bias = mlp_back(cotangent, w_out, slope)
    g_w_in = contract_rows(act_three, d_pre).astype(BF)
    d_pre, g_w_in = sync(d_pre, g_w_in)
    g_w_in = to_dp(g_w_in)
    d_act_three = product_t(d_pre, w_in)
    g_gain_three = jnp.sum(d_act_three * unit_three, axis=0)
    g_bias_three = jnp.sum(d_act_three, axis=0)
    d_resid_three = grad_out + norm_back(unit_three, inv_three, d_act_three * gain_three)

    d_cross_out = d_resid_three.astype(BF)
    d_cross = product_t(d_cross_out, w_cross_out).astype(BF)
    d_cq, d_ck, d_cv = attend_back(
        cross_q, cross_kv, cross_kv, cross_at, HEADS, my_query, patch_key, cross_att, cross_lse, d_cross
    )
    d_act_two = product_t(d_cq, w_cross_q)
    g_gain_two = jnp.sum(d_act_two * unit_two, axis=0)
    g_bias_two = jnp.sum(d_act_two, axis=0)
    d_resid_two = d_resid_three + norm_back(unit_two, inv_two, d_act_two * gain_two)

    d_self_out = d_resid_two.astype(BF)
    d_self = product_t(d_self_out, w_self_out).astype(BF)
    d_self_mine = lax.all_to_all(d_self, "seq", 1, 0, tiled=True)
    g_mid = weight_grads(
        [(self_att, d_self_out), (act_two, d_cq), (patch_all, d_ck), (patch_all, d_cv), (cross_att, d_cross_out)]
    )
    patch_part = (product_t(d_ck, w_cross_kv[:, :width]) + product_t(d_cv, w_cross_kv[:, width:])).astype(BF)
    block_out = (resid_three + product(hid, w_out) + out_bias).astype(BF)
    d_self_mine, g_mid, patch_part, block_out, g_w_out = sync(d_self_mine, g_mid, patch_part, block_out, g_w_out)

    def over_seq(value):
        return exchange_start(value.reshape((ns, -1) + value.shape[1:]), seq)

    g_mid = to_dp(g_mid)
    out_sum, in_sum = over_seq(g_w_out), None
    patch_line = LineSum(patch_part, ns)
    patch_line.start()
    backs = []
    for first in range(0, heads_here, 2):
        back = attend_back(
            qkv, qkv, qkv, self_at, 2, tri_query, tri_key, self_mine, self_lse, d_self_mine, first=first
        )
        if in_sum is None:
            back, d_self_mine, g_w_in, patch_line.moved = sync(back, d_self_mine, g_w_in, patch_line.moved)
            in_sum = over_seq(g_w_in)
            patch_line.start()
        backs.append(back)
    backs, patch_line.moved, out_sum = sync(backs, patch_line.moved, out_sum)
    for _ in range(patch_line.k, ns - 1):
        patch_line.start()
    d_q, d_k, d_v = (jnp.concatenate(p, axis=1) if len(p) > 1 else p[0] for p in zip(*backs))
    d_act_one, g_mod_items = modulate_back(d_q, d_k, d_v, qkv_mine, token_all, tri_col, items)
    d_act_one, g_mod_items, d_q, d_k, d_v, in_sum, patch_line.moved, out_sum = sync(
        d_act_one, g_mod_items, d_q, d_k, d_v, in_sum, patch_line.moved, out_sum
    )

    line = LineSum(d_act_one, ns)
    line.start()
    g_mod = lax.dot_general(
        g_mod_items, cameras.astype(F32), (((0,), (0,)), ((), ())), precision=lax.Precision.HIGHEST
    )
    tail = jnp.concatenate(
        [g_mod.reshape(n_dev, -1)]
        + [v.reshape(n_dev, -1) for v in (g_gain_two, g_bias_two, g_gain_three, g_bias_three, g_out_bias, g_in_bias)],
        axis=1,
    )
    tail = jnp.pad(tail, ((0, 0), (0, extra * w_rows - length))).reshape(n_dev * w_rows, extra).astype(BF)
    g_qkv = weight_grads([(act_one, d_q), (act_one, d_k), (act_one, d_v)])
    g_qkv = jnp.concatenate([g_qkv, tail], axis=1)
    line.moved, g_qkv, in_sum, g_mid = sync(line.moved, g_qkv, in_sum, g_mid)
    g_qkv = to_dp(g_qkv)
    g_mid = over_seq(g_mid)
    line.start()
    patch_grad, g_w_out, g_w_in = patch_line.total(), add_all(out_sum), add_all(in_sum)
    line.moved, patch_grad, g_w_out, g_w_in, g_mid = sync(line.moved, patch_grad, g_w_out, g_w_in, g_mid)
    for _ in range(line.k, ns - 1):
        line.start()
    g_mid = add_all(g_mid)
    line.moved, g_mid, g_qkv = sync(line.moved, g_mid, g_qkv)
    g_qkv = exchange_start(g_qkv.reshape(ns, w_rows, -1), seq)
    d_act_one = line.total()
    unit_own, inv_own = norm_parts(resid_in)
    scale_own = per_item(my_items.reshape(-1, 1), mod_items[:, width:])
    input_grad = d_resid_two + norm_back(unit_own, inv_own, d_act_one * (1.0 + scale_own))
    g_qkv = join([g[None] for g in g_qkv], seq).astype(F32)
    tail = jnp.sum(g_qkv[:, :, 3 * cols_here :], axis=0).reshape(-1)
    g_mod = tail[:mod_n].reshape(mod_weight.shape)
    parts = [tail[mod_n + n * own : mod_n + (n + 1) * own] for n in range(5)]
    g_in_bias = tail[mod_n + 5 * own : length]
    g_qkv = g_qkv[:, :, : 3 * cols_here].reshape(ns, w_rows, 3, cols_here)
    g_qkv = g_qkv.transpose(1, 2, 0, 3).reshape(qkv_weight.shape)
    return (
        block_out,
        input_grad,
        patch_grad,
        g_mod,
        g_qkv,
        g_mid[:, :width],
        parts[0],
        parts[1],
        g_mid[:, width : 2 * width],
        g_mid[:, 2 * width : 4 * width],
        g_mid[:, 4 * width :],
        parts[2],
        parts[3],
        g_w_in,
        g_in_bias,
        g_w_out,
        parts[4],
    )


def solution(mesh):
    nd, ns = mesh.shape["dp"], mesh.shape["seq"]
    rows2, rows1 = P(ALL, None), P(ALL)
    placed = (rows2, rows2, P("dp", None), P("dp"), P("dp"), rows2, rows2, rows2, rows1, rows1, rows2, rows2, rows2, rows1, rows1, rows2, rows1, rows2, rows1, rows2)
    given = (rows2, rows2, rows2, rows2, rows2, rows2, rows1, rows1, rows2, rows2, rows2, rows1, rows1, rows2, rows1, rows2, rows1)

    def shards(*args):
        return block(nd, ns, *args)

    return jax.shard_map(shards, mesh=mesh, in_specs=placed, out_specs=given, check_vma=False)
```

```python
import functools
import math

import jax
import jax.numpy as jnp
from jax import lax
from jax.experimental import pallas as pl
from jax.experimental.pallas import tpu as pltpu
from jax.sharding import PartitionSpec as P

HEADS = 16
HEAD = 64
PAIR = 2 * HEAD
BF = jnp.bfloat16
F32 = jnp.float32
LOG2E = math.log2(math.e)
ALL = ("dp", "seq")
SOFT = LOG2E / math.sqrt(HEAD)
NEG = -1e30
VMEM_LIMIT = 56 * 1024 * 1024


def product(a, b):
    return jnp.dot(a, b, preferred_element_type=F32)


def product_t(a, b):
    return lax.dot_general(a, b, (((1,), (1,)), ((), ())), preferred_element_type=F32)


def contract_rows(a, b):
    return lax.dot_general(a, b, (((0,), (0,)), ((), ())), preferred_element_type=F32)


SHORT = pl.CostEstimate(flops=1, bytes_accessed=1, transcendentals=0)


def kernel_params():
    return pltpu.CompilerParams(vmem_limit_bytes=VMEM_LIMIT)


def query_tags(ids, items):
    slot = lax.broadcasted_iota(jnp.int32, (ids.shape[0], PAIR), 1) % HEAD
    return jnp.where((slot != ids[:, None]) & (slot < items), NEG, 0.0).astype(BF)


def key_tags(ids):
    slot = lax.broadcasted_iota(jnp.int32, (ids.shape[0], PAIR), 1) % HEAD
    return jnp.where(slot == ids[:, None], 1.0, 0.0).astype(BF)


def in_head(value, h, other):
    lane = lax.broadcasted_iota(jnp.int32, value.shape, 1)
    return jnp.where((lane < HEAD) if h == 0 else (lane >= HEAD), value, other)


def only_head(value, h):
    return in_head(value, h, jnp.zeros_like(value))


def attend_kernel(q_ref, k_ref, v_ref, qtag_ref, ktag_ref, o_ref, lse_ref, key_ref, val_ref, *, heads):
    qb = q_ref.shape[0]

    @pl.when(pl.program_id(1) == 0)
    def _():
        for p in range(heads // 2):
            lanes = slice(p * PAIR, (p + 1) * PAIR)
            for h in range(2):
                key_ref[2 * p + h] = in_head(k_ref[:, lanes], h, ktag_ref[...])
                val_ref[2 * p + h] = in_head(v_ref[:, lanes], h, jnp.ones_like(ktag_ref))

    for p in range(heads // 2):
        lanes = slice(p * PAIR, (p + 1) * PAIR)
        sums, tops = [], []
        for h in range(2):
            scores = product_t(in_head(q_ref[:, lanes], h, qtag_ref[...]), key_ref[2 * p + h])
            top = jnp.max(scores, axis=1, keepdims=True)
            probs = jnp.exp2((scores - top) * SOFT).astype(BF)
            sums.append(product(probs, val_ref[2 * p + h]))
            tops.append(top)
        first = lax.broadcasted_iota(jnp.int32, (qb, PAIR), 1) < HEAD
        total = jnp.where(first, pltpu.roll(sums[0], HEAD, 1), pltpu.roll(sums[1], HEAD, 1))
        o_ref[:, lanes] = (jnp.where(first, sums[0], sums[1]) / total).astype(BF)
        lse = (jnp.where(first, tops[0], tops[1]) * SOFT + jnp.log2(total)).T
        lse_ref[p] = jnp.concatenate([lse[0:1], lse[HEAD : HEAD + 1]], axis=0)


def attend(q, k, v, starts, heads, q_tags, k_tags):
    nq, nk = q.shape[0], k.shape[0]
    step = min(4, heads)
    cols = step * HEAD
    qb = min(256 * max(1, 2048 // nk), nq)
    q_off, k_off, v_off = (s // cols for s in starts)
    return pl.pallas_call(
        functools.partial(attend_kernel, heads=step),
        grid=(heads // step, nq // qb),
        in_specs=[
            pl.BlockSpec((qb, cols), lambda p, i: (i, q_off + p)),
            pl.BlockSpec((nk, cols), lambda p, i: (0, k_off + p)),
            pl.BlockSpec((nk, cols), lambda p, i: (0, v_off + p)),
            pl.BlockSpec((qb, PAIR), lambda p, i: (i, 0)),
            pl.BlockSpec((nk, PAIR), lambda p, i: (0, 0)),
        ],
        out_specs=[
            pl.BlockSpec((qb, cols), lambda p, i: (i, p)),
            pl.BlockSpec((step // 2, 2, qb), lambda p, i: (p, 0, i)),
        ],
        out_shape=[
            jax.ShapeDtypeStruct((nq, heads * HEAD), BF),
            jax.ShapeDtypeStruct((heads // 2, 2, nq), F32),
        ],
        scratch_shapes=[pltpu.VMEM((step, nk, PAIR), BF), pltpu.VMEM((step, nk, PAIR), BF)],
        compiler_params=kernel_params(),
        cost_estimate=SHORT,
        name="attend",
    )(q, k, v, q_tags, k_tags)


def attend_back_kernel(q_ref, k_ref, v_ref, do_ref, o_ref, lse_ref, qtag_ref, ktag_ref, dq_ref, dk_ref, dv_ref, key_ref, kt_ref, dk_sum, dv_sum, *, kb):
    i = pl.program_id(1)
    nk = k_ref.shape[0]

    @pl.when(i == 0)
    def _():
        kt_ref[...] = k_ref[...].T
        for h in range(2):
            key_ref[h] = in_head(k_ref[...], h, ktag_ref[...])
        dk_sum[...] = jnp.zeros(dk_sum.shape, F32)
        dv_sum[...] = jnp.zeros(dv_sum.shape, F32)

    q, do = q_ref[...], do_ref[...]
    both = (do.astype(F32) * o_ref[...].astype(F32)).T
    q_own = [only_head(q, h) for h in range(2)]
    do_own = [only_head(do, h) for h in range(2)]
    q_tag = [in_head(q, h, qtag_ref[...]) for h in range(2)]
    delta = [jnp.sum(both[h * HEAD : (h + 1) * HEAD], axis=0, keepdims=True) for h in range(2)]
    dq = [None, None]
    for j in range(nk // kb):
        rows = slice(j * kb, (j + 1) * kb)
        probs_low, grads_low = [], []
        for h in range(2):
            scores = product_t(key_ref[h, rows, :], q_tag[h])
            probs = jnp.exp2(scores * SOFT - lse_ref[0, h : h + 1, :])
            grad_probs = product_t(v_ref[rows, :], do_own[h])
            grads_low.append((probs * (grad_probs - delta[h])).astype(BF))
            probs_low.append(probs.astype(BF))
            term = product(kt_ref[h * HEAD : (h + 1) * HEAD, rows], grads_low[h])
            dq[h] = term if dq[h] is None else dq[h] + term
        dv_sum[rows, :] += product(jnp.concatenate(probs_low, axis=1), jnp.concatenate(do_own, axis=0))
        dk_sum[rows, :] += product(jnp.concatenate(grads_low, axis=1), jnp.concatenate(q_own, axis=0))
    dq_ref[...] = (jnp.concatenate(dq, axis=0) * (1.0 / math.sqrt(HEAD))).T.astype(BF)

    @pl.when(i == pl.num_programs(1) - 1)
    def _():
        dk_ref[...] = (dk_sum[...] * (1.0 / math.sqrt(HEAD))).astype(BF)
        dv_ref[...] = dv_sum[...].astype(BF)


def attend_back(q, k, v, starts, heads, q_tags, k_tags, out, lse, grad_out, first=0):
    nq, nk = q.shape[0], k.shape[0]
    pairs = heads // 2
    qb, kb = min(512, nq), min(2048, nk)
    base = first // 2
    q_off, k_off, v_off = (s // PAIR + base for s in starts)
    mine = pl.BlockSpec((qb, PAIR), lambda p, i: (i, p + base))
    return pl.pallas_call(
        functools.partial(attend_back_kernel, kb=kb),
        grid=(pairs, nq // qb),
        in_specs=[
            pl.BlockSpec((qb, PAIR), lambda p, i: (i, q_off + p)),
            pl.BlockSpec((nk, PAIR), lambda p, i: (0, k_off + p)),
            pl.BlockSpec((nk, PAIR), lambda p, i: (0, v_off + p)),
            mine,
            mine,
            pl.BlockSpec((1, 2, qb), lambda p, i: (p + base, 0, i)),
            pl.BlockSpec((qb, PAIR), lambda p, i: (i, 0)),
            pl.BlockSpec((nk, PAIR), lambda p, i: (0, 0)),
        ],
        out_specs=[
            pl.BlockSpec((qb, PAIR), lambda p, i: (i, p)),
            pl.BlockSpec((nk, PAIR), lambda p, i: (0, p)),
            pl.BlockSpec((nk, PAIR), lambda p, i: (0, p)),
        ],
        out_shape=[
            jax.ShapeDtypeStruct((nq, pairs * PAIR), BF),
            jax.ShapeDtypeStruct((nk, pairs * PAIR), BF),
            jax.ShapeDtypeStruct((nk, pairs * PAIR), BF),
        ],
        scratch_shapes=[
            pltpu.VMEM((2, nk, PAIR), BF),
            pltpu.VMEM((PAIR, nk), BF),
            pltpu.VMEM((nk, PAIR), F32),
            pltpu.VMEM((nk, PAIR), F32),
        ],
        compiler_params=kernel_params(),
        cost_estimate=SHORT,
        name="attend_back",
    )(q, k, v, grad_out, out, lse, q_tags, k_tags)


def mlp_up_kernel(a_ref, w_ref, b_ref, hid_ref, slope_ref):
    pre = product(a_ref[...], w_ref[...]) + b_ref[...]
    cdf = 0.5 * (1.0 + lax.erf(pre * (1.0 / math.sqrt(2.0))))
    density = jnp.exp(-0.5 * pre * pre) * (1.0 / math.sqrt(2.0 * math.pi))
    hid_ref[...] = (pre * cdf).astype(BF)
    slope_ref[...] = (cdf + pre * density).astype(BF)


def mlp_up(act, w, bias):
    rows, ff = act.shape[0], w.shape[1]
    cb = 1024
    block = pl.BlockSpec((rows, cb), lambda g: (0, g))
    return pl.pallas_call(
        mlp_up_kernel,
        grid=(ff // cb,),
        in_specs=[
            pl.BlockSpec(act.shape, lambda g: (0, 0)),
            pl.BlockSpec((w.shape[0], cb), lambda g: (0, g)),
            pl.BlockSpec((1, cb), lambda g: (0, g)),
        ],
        out_specs=[block, block],
        out_shape=[jax.ShapeDtypeStruct((rows, ff), BF)] * 2,
        compiler_params=kernel_params(),
        cost_estimate=SHORT,
        name="mlp_up",
    )(act, w, bias)


def mlp_back_kernel(g_ref, w_ref, slope_ref, out_ref, sum_ref):
    grad = product_t(g_ref[...], w_ref[...]) * slope_ref[...].astype(F32)
    low = grad.astype(BF)
    out_ref[...] = low
    sum_ref[...] = jnp.sum(low.astype(F32), axis=0, keepdims=True)


def mlp_back(grad, w, slope):
    rows, ff = slope.shape
    cb = 1024
    block = pl.BlockSpec((rows, cb), lambda g: (0, g))
    return pl.pallas_call(
        mlp_back_kernel,
        grid=(ff // cb,),
        in_specs=[
            pl.BlockSpec(grad.shape, lambda g: (0, 0)),
            pl.BlockSpec((cb, w.shape[1]), lambda g: (g, 0)),
            block,
        ],
        out_specs=[block, pl.BlockSpec((1, cb), lambda g: (0, g))],
        out_shape=[jax.ShapeDtypeStruct((rows, ff), BF), jax.ShapeDtypeStruct((1, ff), F32)],
        compiler_params=kernel_params(),
        cost_estimate=SHORT,
        name="mlp_back",
    )(grad, w, slope)


def norm_parts(values):
    centre = values - jnp.mean(values, axis=-1, keepdims=True)
    spread = jnp.mean(centre * centre, axis=-1, keepdims=True)
    inverse = lax.rsqrt(spread + 1e-05)
    return centre * inverse, inverse


def norm_back(unit, inverse, grad):
    return inverse * (
        grad
        - jnp.mean(grad, axis=-1, keepdims=True)
        - unit * jnp.mean(grad * unit, axis=-1, keepdims=True)
    )


def per_item(ids, rows):
    out = jnp.broadcast_to(rows[0:1, :], (ids.shape[0], rows.shape[1]))
    for n in range(1, rows.shape[0]):
        out = jnp.where(ids == n, rows[n : n + 1, :], out)
    return out


def modulate_kernel(me_ref, *refs, per, offsets):
    pieces, (id_ref, mod_ref, out_ref, x_ref) = refs[:-4], refs[-4:]
    width = out_ref.shape[1]
    block = pl.program_id(0) // per
    for off, piece in zip(offsets, pieces):
        @pl.when(me_ref[0] + off == block)
        def _():
            x_ref[...] = piece[...]

    unit, _ = norm_parts(x_ref[...].astype(F32))
    ids = id_ref[...]
    shift = per_item(ids, mod_ref[:, :width])
    scale = per_item(ids, mod_ref[:, width:])
    out_ref[...] = (unit * (1.0 + scale) + shift).astype(BF)


def modulate(pieces, offsets, me, ids, mod_items):
    rows, width = pieces[0].shape
    rb = min(512, rows)
    per = rows // rb
    total = ids.shape[0]
    block = pl.BlockSpec((rb, width), lambda i, me: (i, 0))
    return pl.pallas_call(
        functools.partial(modulate_kernel, per=per, offsets=offsets),
        grid_spec=pltpu.PrefetchScalarGridSpec(
            num_scalar_prefetch=1,
            grid=(total // rb,),
            in_specs=[
                pl.BlockSpec((rb, width), lambda i, me, off=off: (jnp.where(me[0] + off == i // per, i % per, 0), 0))
                for off in offsets
            ]
            + [
                pl.BlockSpec((rb, 1), lambda i, me: (i, 0)),
                pl.BlockSpec(mod_items.shape, lambda i, me: (0, 0)),
            ],
            out_specs=[block, block],
        ),
        out_shape=[jax.ShapeDtypeStruct((total, width), BF)] * 2,
        compiler_params=kernel_params(),
        cost_estimate=SHORT,
        name="modulate",
    )(me.reshape(1), *pieces, ids, mod_items)


def modulate_back_kernel(dq_ref, dk_ref, dv_ref, w_ref, x_ref, id_ref, out_ref, sum_ref):
    width = x_ref.shape[1]
    c = dq_ref.shape[1]
    items = sum_ref.shape[0]
    grad = product_t(dq_ref[...], w_ref[:, 0:c])
    grad += product_t(dk_ref[...], w_ref[:, c : 2 * c])
    grad += product_t(dv_ref[...], w_ref[:, 2 * c :])
    out_ref[...] = grad.astype(BF)

    @pl.when(pl.program_id(0) == 0)
    def _():
        sum_ref[...] = jnp.zeros(sum_ref.shape, F32)

    unit, _ = norm_parts(x_ref[...].astype(F32))
    times = grad * unit
    ids = id_ref[...]
    low, high = jnp.min(ids), jnp.max(ids)
    for n in range(items):
        @pl.when((low <= n) & (n <= high))
        def _():
            here = ids == n
            sum_ref[n : n + 1, :width] += jnp.sum(jnp.where(here, grad, 0.0), axis=0, keepdims=True)
            sum_ref[n : n + 1, width:] += jnp.sum(jnp.where(here, times, 0.0), axis=0, keepdims=True)


def modulate_back(d_q, d_k, d_v, w, x, ids, items):
    rows, width = x.shape
    rb = 512
    c = d_q.shape[1]
    part = pl.BlockSpec((rb, c), lambda i: (i, 0))
    return pl.pallas_call(
        modulate_back_kernel,
        grid=(rows // rb,),
        in_specs=[
            part,
            part,
            part,
            pl.BlockSpec(w.shape, lambda i: (0, 0)),
            pl.BlockSpec((rb, width), lambda i: (i, 0)),
            pl.BlockSpec((rb, 1), lambda i: (i, 0)),
        ],
        out_specs=[
            pl.BlockSpec((rb, width), lambda i: (i, 0)),
            pl.BlockSpec((items, 2 * width), lambda i: (0, 0)),
        ],
        out_shape=[jax.ShapeDtypeStruct((rows, width), BF), jax.ShapeDtypeStruct((items, 2 * width), F32)],
        compiler_params=kernel_params(),
        cost_estimate=SHORT,
        name="modulate_back",
    )(d_q, d_k, d_v, w, x, ids)


def grads_kernel(*refs, spans, sources, count):
    g = pl.program_id(0)
    x_refs, y_refs, out_ref, xt_ref = refs[:count], refs[count:-2], refs[-2], refs[-1]
    for i, (start, stop) in enumerate(spans):
        rows = y_refs[i].shape[0]
        if i == 0 or sources[i] != sources[i - 1]:
            @pl.when(g == start)
            def _():
                xt_ref[:, :rows] = x_refs[sources[i]][...].T

        @pl.when((g >= start) & (g < stop))
        def _():
            out_ref[...] = product(xt_ref[:, :rows], y_refs[i][...]).astype(BF)


def weight_grads(pairs):
    flat = [(n, y) for n, (_, ys) in enumerate(pairs) for y in ys]
    width = pairs[0][0].shape[1]
    cb = min(1024, min(y.shape[1] for _, y in flat))
    spans, at = [], 0
    for _, y in flat:
        spans.append((at, at + y.shape[1] // cb))
        at = spans[-1][1]
    in_specs = [pl.BlockSpec(x.shape, lambda g: (0, 0), pipeline_mode=pl.Buffered(1)) for x, _ in pairs]
    for (_, y), (start, stop) in zip(flat, spans):
        in_specs.append(
            pl.BlockSpec((y.shape[0], cb), lambda g, start=start, stop=stop: (0, jnp.clip(g - start, 0, stop - start - 1)))
        )
    longest = max(x.shape[0] for x, _ in pairs)
    return pl.pallas_call(
        functools.partial(grads_kernel, spans=tuple(spans), sources=tuple(n for n, _ in flat), count=len(pairs)),
        grid=(at,),
        in_specs=in_specs,
        out_specs=pl.BlockSpec((width, cb), lambda g: (0, g)),
        scratch_shapes=[pltpu.VMEM((width, longest), BF)],
        out_shape=jax.ShapeDtypeStruct((width, at * cb), BF),
        compiler_params=kernel_params(),
        cost_estimate=SHORT,
        name="weight_grads",
    )(*[x for x, _ in pairs], *[y for _, y in flat])


def bits_of(size):
    return [1 << b for b in range(size.bit_length() - 1)]


class Axis:
    def __init__(self, name, length, size, me, flip):
        self.name, self.length, self.size, self.me, self.flip = name, length, size, me, flip

    def send(self, value, m):
        return lax.ppermute(value, self.name, [(r, r ^ self.flip(m)) for r in range(self.length)])

    def mine(self, bit):
        return (self.me // bit) % 2


def pick(value, index, where):
    return lax.dynamic_index_in_dim(value, index, where, keepdims=False)


def sync(*values):
    return lax.optimization_barrier(values)


def natural(pieces, axis):
    pieces = list(pieces)
    for bit in bits_of(axis.size):
        flip = axis.mine(bit) == 1
        out = list(pieces)
        for m in range(axis.size):
            if not m & bit:
                out[m] = jnp.where(flip, pieces[m | bit], pieces[m])
                out[m | bit] = jnp.where(flip, pieces[m], pieces[m | bit])
        pieces = out
    return pieces


def join(pieces, axis):
    if isinstance(pieces, dict):
        pieces = [pieces[m] for m in range(axis.size)]
    return jnp.concatenate(natural(pieces, axis), axis=0)


def exchange_start(blocks, axis):
    return [pick(blocks, axis.me ^ m, 0) if m == 0 else axis.send(pick(blocks, axis.me ^ m, 0), m) for m in range(axis.size)]


def xor_start(value, axis):
    return [value] + [axis.send(value, m) for m in range(1, axis.size)]


def double_start(have, bit, axis):
    return {**have, **{m | bit: axis.send(v, bit) for m, v in have.items()}}


class LineSum:
    def __init__(self, parts, ns):
        self.parts, self.ns, self.k = parts, ns, 0
        self.moved = None

    def chunk(self, d):
        rows = self.parts.shape[0] // self.ns
        return lax.dynamic_slice_in_dim(self.parts, jnp.clip(d, 0, self.ns - 1) * rows, rows).astype(F32)

    def start(self):
        self.k += 1
        k, ns, me = self.k, self.ns, lax.axis_index("seq")
        above, below = self.chunk(me + ns - k), self.chunk(me - ns + k)
        if self.moved is not None:
            above, below = above + self.moved[0].astype(F32), below + self.moved[1].astype(F32)
        self.moved = (
            lax.ppermute(above.astype(BF), "seq", [(r, r + 1) for r in range(k)]),
            lax.ppermute(below.astype(BF), "seq", [(ns - 1 - r, ns - 2 - r) for r in range(k)]),
        )

    def total(self):
        return self.chunk(lax.axis_index("seq")) + self.moved[0].astype(F32) + self.moved[1].astype(F32)


def line_step(up, down, ns):
    return (
        lax.ppermute(up, "seq", [(r, r + 1) for r in range(ns - 1)]),
        lax.ppermute(down, "seq", [(r + 1, r) for r in range(ns - 1)]),
    )


def line_join(ups, downs, ns):
    ring = [ups[0]] + [downs[r] + ups[ns - r] for r in range(1, ns)]
    rows = ups[0].shape[0]
    first = (ns - lax.axis_index("seq")) % ns
    return lax.dynamic_slice_in_dim(jnp.concatenate(ring + ring[:-1], axis=0), first * rows, ns * rows)


def add_all(pieces, dtype=F32):
    total = pieces[0].astype(F32)
    for value in pieces[1:]:
        total = total + value.astype(F32)
    return total.astype(dtype)


def to_dp(whole):
    return lax.psum_scatter(whole, "dp", scatter_dimension=0, tiled=True)


def block(nd, ns, tokens, patches, cameras, tri_items, patch_items, mod_weight, qkv_weight, self_out_weight, norm2_gain, norm2_bias, cross_q_weight, cross_kv_weight, cross_out_weight, norm3_gain, norm3_bias, mlp_in_weight, mlp_in_bias, mlp_out_weight, mlp_out_bias, cotangent):
    rows, width = tokens.shape
    heads_here = HEADS // ns
    cols_here = width // ns
    items = cameras.shape[0]
    w_rows = qkv_weight.shape[0]
    n_dev = nd * ns
    seq = Axis("seq", ns, ns, lax.axis_index("seq"), lambda m: m)

    def over_dp(held):
        return lax.all_gather(join(held, seq), "dp", axis=0, tiled=True)

    down_bits = bits_of(ns)[::-1]

    bundle = {0: jnp.concatenate([self_out_weight, cross_q_weight, cross_kv_weight, cross_out_weight], axis=1)}
    small = jnp.concatenate(
        [mod_weight.reshape(-1), norm2_gain, norm2_bias, norm3_gain, norm3_bias, mlp_out_bias, mlp_in_bias]
    )
    length = small.shape[0]
    extra = -(-length // w_rows)
    extra += -extra % 128
    small = jnp.pad(small, (0, extra * w_rows - length)).reshape(w_rows, extra)
    cut = qkv_weight.reshape(w_rows, 3, ns, cols_here).transpose(2, 0, 1, 3).reshape(ns, w_rows, 3 * cols_here)
    cut = jnp.concatenate([cut, jnp.broadcast_to(small[None], (ns, w_rows, extra))], axis=2)

    ups, downs = [tokens], [tokens]
    todo = list(down_bits)
    for k in range(1, ns):
        up, down = line_step(ups[-1], downs[-1], ns)
        if k == 1:
            cut = exchange_start(cut, seq)
            up, down, cut = sync(up, down, cut)
            cut = lax.all_gather(join(cut, seq), "dp", axis=0, tiled=True)
        else:
            if todo:
                bundle = double_start(bundle, todo.pop(0), seq)
                up, down, bundle = sync(up, down, bundle)
                if not todo:
                    bundle = over_dp(bundle)
            else:
                up, down = sync(up, down)
        ups.append(up)
        downs.append(down)
    if len(todo) or ns == 2:
        while todo:
            bundle = double_start(bundle, todo.pop(0), seq)
        bundle = over_dp(bundle)
    ups, downs, cut, patches, mlp_in_weight = sync(ups, downs, cut, patches, mlp_in_weight)
    qkv_mine = cut[:, : 3 * cols_here]
    small = cut[:, 3 * cols_here :].reshape(n_dev, -1)
    mod_n = mod_weight.size
    own = norm2_gain.shape[0]
    mod_full = small[:, :mod_n].reshape(-1, mod_weight.shape[1])
    vectors = [small[:, mod_n + n * own : mod_n + (n + 1) * own].reshape(1, -1).astype(F32) for n in range(5)]
    gain_two, bias_two, gain_three, bias_three, out_bias = vectors
    in_bias = small[:, mod_n + 5 * own : length].reshape(1, -1).astype(F32)

    tri_col = tri_items.reshape(-1, 1)
    tri_query, tri_key = query_tags(tri_items, items), key_tags(tri_items)
    my_items = lax.dynamic_slice_in_dim(tri_items, seq.me * rows, rows)
    my_query, patch_key = query_tags(my_items, items), key_tags(patch_items)

    mod_items = product_t(cameras, mod_full)
    patch_ups, patch_downs = [patches], [patches]

    def patch_step():
        if len(patch_ups) < ns:
            up, down = line_step(patch_ups[-1], patch_downs[-1], ns)
            patch_ups.append(up)
            patch_downs.append(down)

    patch_step()
    w_in = double_start({0: mlp_in_weight}, down_bits[0], seq)
    steps = range(1, ns)
    act_one, token_all = modulate(
        [tokens] + ups[1:] + downs[1:], [0] + [-k for k in steps] + list(steps), seq.me, tri_col, mod_items
    )
    act_one, w_in, patch_ups[-1], patch_downs[-1] = sync(act_one, w_in, patch_ups[-1], patch_downs[-1])
    for bit in down_bits[1:]:
        w_in = double_start(w_in, bit, seq)
    patch_step()
    qkv = product(act_one, qkv_mine).astype(BF)
    qkv, w_in, mlp_out_weight, patch_ups[-1], patch_downs[-1] = sync(
        qkv, w_in, mlp_out_weight, patch_ups[-1], patch_downs[-1]
    )
    w_in = over_dp(w_in)
    while len(patch_ups) < ns:
        patch_step()
    w_out = double_start({0: mlp_out_weight}, down_bits[0], seq)
    self_at = (0, cols_here, 2 * cols_here)
    self_mine, self_lse = attend(qkv, qkv, qkv, self_at, heads_here, tri_query, tri_key)
    self_mine, bundle, patch_ups, patch_downs, w_out = sync(self_mine, bundle, patch_ups, patch_downs, w_out)
    w_self_out = bundle[:, :width]
    w_cross_q = bundle[:, width : 2 * width]
    w_cross_kv = bundle[:, 2 * width : 4 * width]
    w_cross_out = bundle[:, 4 * width :]
    self_att = lax.all_to_all(self_mine, "seq", 0, 1, tiled=True)
    patch_all = line_join(patch_ups, patch_downs, ns)
    cross_kv = product(patch_all, w_cross_kv).astype(BF)
    self_att, cross_kv = sync(self_att, cross_kv)
    for bit in down_bits[1:]:
        w_out = double_start(w_out, bit, seq)
    resid_in = tokens.astype(F32)
    resid_two = resid_in + product(self_att, w_self_out)

    unit_two, inv_two = norm_parts(resid_two)
    act_two = (unit_two * gain_two + bias_two).astype(BF)
    cross_q = product(act_two, w_cross_q).astype(BF)
    cross_q, w_out = sync(cross_q, w_out)
    w_out = over_dp(w_out)
    cross_at = (0, 0, width)
    cross_att, cross_lse = attend(cross_q, cross_kv, cross_kv, cross_at, HEADS, my_query, patch_key)
    resid_three = resid_two + product(cross_att, w_cross_out)

    unit_three, inv_three = norm_parts(resid_three)
    act_three = (unit_three * gain_three + bias_three).astype(BF)
    act_three, w_in = sync(act_three, w_in)
    hid, slope = mlp_up(act_three, w_in, in_bias)

    g_w_out = contract_rows(hid, cotangent).astype(BF)
    slope, g_w_out, w_out = sync(slope, g_w_out, w_out)
    g_w_out = to_dp(g_w_out)
    grad_out = cotangent.astype(F32)
    g_out_bias = jnp.sum(grad_out, axis=0)
    d_pre, g_in_bias = mlp_back(cotangent, w_out, slope)
    g_w_in = contract_rows(act_three, d_pre).astype(BF)
    d_pre, g_w_in = sync(d_pre, g_w_in)
    g_w_in = to_dp(g_w_in)
    d_act_three = product_t(d_pre, w_in)
    g_gain_three = jnp.sum(d_act_three * unit_three, axis=0)
    g_bias_three = jnp.sum(d_act_three, axis=0)
    d_resid_three = grad_out + norm_back(unit_three, inv_three, d_act_three * gain_three)

    d_cross_out = d_resid_three.astype(BF)
    d_cross = product_t(d_cross_out, w_cross_out).astype(BF)
    d_cq, d_ck, d_cv = attend_back(
        cross_q, cross_kv, cross_kv, cross_at, HEADS, my_query, patch_key, cross_att, cross_lse, d_cross
    )
    d_act_two = product_t(d_cq, w_cross_q)
    g_gain_two = jnp.sum(d_act_two * unit_two, axis=0)
    g_bias_two = jnp.sum(d_act_two, axis=0)
    d_resid_two = d_resid_three + norm_back(unit_two, inv_two, d_act_two * gain_two)

    d_self_out = d_resid_two.astype(BF)
    d_self = product_t(d_self_out, w_self_out).astype(BF)
    d_self_mine = lax.all_to_all(d_self, "seq", 1, 0, tiled=True)

    def over_seq(value):
        return exchange_start(value.reshape((ns, -1) + value.shape[1:]), seq)

    g_mid = weight_grads(
        [(self_att, [d_self_out]), (act_two, [d_cq]), (patch_all, [d_ck, d_cv]), (cross_att, [d_cross_out])]
    )
    patch_part = (product_t(d_ck, w_cross_kv[:, :width]) + product_t(d_cv, w_cross_kv[:, width:])).astype(BF)
    block_out = (resid_three + product(hid, w_out) + out_bias).astype(BF)
    d_self_mine, g_mid, patch_part, block_out, g_w_out = sync(d_self_mine, g_mid, patch_part, block_out, g_w_out)
    g_mid = to_dp(g_mid)
    out_sum, in_sum = over_seq(g_w_out), None
    patch_line = LineSum(patch_part, ns)
    patch_line.start()
    backs = []
    for first in range(0, heads_here, 2):
        back = attend_back(
            qkv, qkv, qkv, self_at, 2, tri_query, tri_key, self_mine, self_lse, d_self_mine, first=first
        )
        if in_sum is None:
            back, d_self_mine, g_w_in, patch_line.moved = sync(back, d_self_mine, g_w_in, patch_line.moved)
            in_sum = over_seq(g_w_in)
            patch_line.start()
        backs.append(back)
    backs, patch_line.moved, out_sum, in_sum = sync(backs, patch_line.moved, out_sum, in_sum)
    for _ in range(patch_line.k, ns - 1):
        patch_line.start()
    d_q, d_k, d_v = (jnp.concatenate(p, axis=1) if len(p) > 1 else p[0] for p in zip(*backs))
    d_act_one, g_mod_items = modulate_back(d_q, d_k, d_v, qkv_mine, token_all, tri_col, items)
    d_act_one, g_mod_items, d_q, d_k, d_v, in_sum, patch_line.moved, out_sum = sync(
        d_act_one, g_mod_items, d_q, d_k, d_v, in_sum, patch_line.moved, out_sum
    )

    line = LineSum(d_act_one, ns)
    line.start()
    g_mod = lax.dot_general(
        g_mod_items, cameras.astype(F32), (((0,), (0,)), ((), ())), precision=lax.Precision.HIGHEST
    )
    tail = jnp.concatenate(
        [g_mod.reshape(n_dev, -1)]
        + [v.reshape(n_dev, -1) for v in (g_gain_two, g_bias_two, g_gain_three, g_bias_three, g_out_bias, g_in_bias)],
        axis=1,
    )
    tail = jnp.pad(tail, ((0, 0), (0, extra * w_rows - length))).reshape(n_dev * w_rows, extra).astype(BF)
    g_qkv = weight_grads([(act_one, [d_q, d_k, d_v])])
    g_qkv = jnp.concatenate([g_qkv, tail], axis=1)
    line.moved, g_qkv, in_sum, g_mid = sync(line.moved, g_qkv, in_sum, g_mid)
    g_qkv = to_dp(g_qkv)
    g_mid = over_seq(g_mid)
    line.start()
    g_mid[1], patch_line.moved, out_sum, in_sum = sync(g_mid[1], patch_line.moved, out_sum, in_sum)
    patch_grad, g_w_out, g_w_in = patch_line.total(), add_all(out_sum), add_all(in_sum)
    line.moved, patch_grad, g_w_out, g_w_in, g_mid = sync(line.moved, patch_grad, g_w_out, g_w_in, g_mid)
    for _ in range(line.k, ns - 1):
        line.start()
    g_mid = add_all(g_mid)
    line.moved, g_mid, g_qkv = sync(line.moved, g_mid, g_qkv)
    g_qkv = exchange_start(g_qkv.reshape(ns, w_rows, -1), seq)
    d_act_one = line.total()
    unit_own, inv_own = norm_parts(resid_in)
    scale_own = per_item(my_items.reshape(-1, 1), mod_items[:, width:])
    input_grad = d_resid_two + norm_back(unit_own, inv_own, d_act_one * (1.0 + scale_own))
    g_qkv = join([g[None] for g in g_qkv], seq).astype(F32)
    tail = jnp.sum(g_qkv[:, :, 3 * cols_here :], axis=0).reshape(-1)
    g_mod = tail[:mod_n].reshape(mod_weight.shape)
    parts = [tail[mod_n + n * own : mod_n + (n + 1) * own] for n in range(5)]
    g_in_bias = tail[mod_n + 5 * own : length]
    g_qkv = g_qkv[:, :, : 3 * cols_here].reshape(ns, w_rows, 3, cols_here)
    g_qkv = g_qkv.transpose(1, 2, 0, 3).reshape(qkv_weight.shape)
    return (
        block_out,
        input_grad,
        patch_grad,
        g_mod,
        g_qkv,
        g_mid[:, :width],
        parts[0],
        parts[1],
        g_mid[:, width : 2 * width],
        g_mid[:, 2 * width : 4 * width],
        g_mid[:, 4 * width :],
        parts[2],
        parts[3],
        g_w_in,
        g_in_bias,
        g_w_out,
        parts[4],
    )


def solution(mesh):
    nd, ns = mesh.shape["dp"], mesh.shape["seq"]
    rows2, rows1 = P(ALL, None), P(ALL)
    placed = (rows2, rows2, P("dp", None), P("dp"), P("dp"), rows2, rows2, rows2, rows1, rows1, rows2, rows2, rows2, rows1, rows1, rows2, rows1, rows2, rows1, rows2)
    given = (rows2, rows2, rows2, rows2, rows2, rows2, rows1, rows1, rows2, rows2, rows2, rows1, rows1, rows2, rows1, rows2, rows1)

    def shards(*args):
        return block(nd, ns, *args)

    return jax.shard_map(shards, mesh=mesh, in_specs=placed, out_specs=given, check_vma=False)
```

```python
import functools
import math

import jax
import jax.numpy as jnp
from jax import lax
from jax.experimental import pallas as pl
from jax.experimental.pallas import tpu as pltpu
from jax.sharding import PartitionSpec as P

HEADS = 16
HEAD = 64
PAIR = 2 * HEAD
BF = jnp.bfloat16
F32 = jnp.float32
LOG2E = math.log2(math.e)
ALL = ("dp", "seq")
SOFT = LOG2E / math.sqrt(HEAD)
NEG = -1e30
VMEM_LIMIT = 56 * 1024 * 1024


def product(a, b):
    return jnp.dot(a, b, preferred_element_type=F32)


def product_t(a, b):
    return lax.dot_general(a, b, (((1,), (1,)), ((), ())), preferred_element_type=F32)


def contract_rows(a, b):
    return lax.dot_general(a, b, (((0,), (0,)), ((), ())), preferred_element_type=F32)


SHORT = pl.CostEstimate(flops=1, bytes_accessed=1, transcendentals=0)


def kernel_params():
    return pltpu.CompilerParams(vmem_limit_bytes=VMEM_LIMIT)


def query_tags(ids, items):
    slot = lax.broadcasted_iota(jnp.int32, (ids.shape[0], PAIR), 1) % HEAD
    return jnp.where((slot != ids[:, None]) & (slot < items), NEG, 0.0).astype(BF)


def key_tags(ids):
    slot = lax.broadcasted_iota(jnp.int32, (ids.shape[0], PAIR), 1) % HEAD
    return jnp.where(slot == ids[:, None], 1.0, 0.0).astype(BF)


def in_head(value, h, other):
    lane = lax.broadcasted_iota(jnp.int32, value.shape, 1)
    return jnp.where((lane < HEAD) if h == 0 else (lane >= HEAD), value, other)


def only_head(value, h):
    return in_head(value, h, jnp.zeros_like(value))


def attend_kernel(q_ref, k_ref, v_ref, qtag_ref, ktag_ref, o_ref, lse_ref, key_ref, val_ref, *, heads):
    qb = q_ref.shape[0]

    @pl.when(pl.program_id(1) == 0)
    def _():
        for p in range(heads // 2):
            lanes = slice(p * PAIR, (p + 1) * PAIR)
            for h in range(2):
                key_ref[2 * p + h] = in_head(k_ref[:, lanes], h, ktag_ref[...])
                val_ref[2 * p + h] = in_head(v_ref[:, lanes], h, jnp.ones_like(ktag_ref))

    for p in range(heads // 2):
        lanes = slice(p * PAIR, (p + 1) * PAIR)
        sums, tops = [], []
        for h in range(2):
            scores = product_t(in_head(q_ref[:, lanes], h, qtag_ref[...]), key_ref[2 * p + h])
            top = jnp.max(scores, axis=1, keepdims=True)
            probs = jnp.exp2((scores - top) * SOFT).astype(BF)
            sums.append(product(probs, val_ref[2 * p + h]))
            tops.append(top)
        first = lax.broadcasted_iota(jnp.int32, (qb, PAIR), 1) < HEAD
        total = jnp.where(first, pltpu.roll(sums[0], HEAD, 1), pltpu.roll(sums[1], HEAD, 1))
        o_ref[:, lanes] = (jnp.where(first, sums[0], sums[1]) / total).astype(BF)
        lse = (jnp.where(first, tops[0], tops[1]) * SOFT + jnp.log2(total)).T
        lse_ref[p] = jnp.concatenate([lse[0:1], lse[HEAD : HEAD + 1]], axis=0)


def attend(q, k, v, starts, heads, q_tags, k_tags):
    nq, nk = q.shape[0], k.shape[0]
    step = min(4, heads)
    cols = step * HEAD
    qb = min(256 * max(1, 2048 // nk), nq)
    q_off, k_off, v_off = (s // cols for s in starts)
    return pl.pallas_call(
        functools.partial(attend_kernel, heads=step),
        grid=(heads // step, nq // qb),
        in_specs=[
            pl.BlockSpec((qb, cols), lambda p, i: (i, q_off + p)),
            pl.BlockSpec((nk, cols), lambda p, i: (0, k_off + p)),
            pl.BlockSpec((nk, cols), lambda p, i: (0, v_off + p)),
            pl.BlockSpec((qb, PAIR), lambda p, i: (i, 0)),
            pl.BlockSpec((nk, PAIR), lambda p, i: (0, 0)),
        ],
        out_specs=[
            pl.BlockSpec((qb, cols), lambda p, i: (i, p)),
            pl.BlockSpec((step // 2, 2, qb), lambda p, i: (p, 0, i)),
        ],
        out_shape=[
            jax.ShapeDtypeStruct((nq, heads * HEAD), BF),
            jax.ShapeDtypeStruct((heads // 2, 2, nq), F32),
        ],
        scratch_shapes=[pltpu.VMEM((step, nk, PAIR), BF), pltpu.VMEM((step, nk, PAIR), BF)],
        compiler_params=kernel_params(),
        cost_estimate=SHORT,
        name="attend",
    )(q, k, v, q_tags, k_tags)


def attend_back_kernel(q_ref, k_ref, v_ref, do_ref, o_ref, lse_ref, qtag_ref, ktag_ref, dq_ref, dk_ref, dv_ref, key_ref, kt_ref, dk_sum, dv_sum, *, kb):
    i = pl.program_id(1)
    nk = k_ref.shape[0]

    @pl.when(i == 0)
    def _():
        kt_ref[...] = k_ref[...].T
        for h in range(2):
            key_ref[h] = in_head(k_ref[...], h, ktag_ref[...])
        dk_sum[...] = jnp.zeros(dk_sum.shape, F32)
        dv_sum[...] = jnp.zeros(dv_sum.shape, F32)

    q, do = q_ref[...], do_ref[...]
    both = (do.astype(F32) * o_ref[...].astype(F32)).T
    q_own = [only_head(q, h) for h in range(2)]
    do_own = [only_head(do, h) for h in range(2)]
    q_tag = [in_head(q, h, qtag_ref[...]) for h in range(2)]
    delta = [jnp.sum(both[h * HEAD : (h + 1) * HEAD], axis=0, keepdims=True) for h in range(2)]
    dq = [None, None]
    for j in range(nk // kb):
        rows = slice(j * kb, (j + 1) * kb)
        probs_low, grads_low = [], []
        for h in range(2):
            scores = product_t(key_ref[h, rows, :], q_tag[h])
            probs = jnp.exp2(scores * SOFT - lse_ref[0, h : h + 1, :])
            grad_probs = product_t(v_ref[rows, :], do_own[h])
            grads_low.append((probs * (grad_probs - delta[h])).astype(BF))
            probs_low.append(probs.astype(BF))
            term = product(kt_ref[h * HEAD : (h + 1) * HEAD, rows], grads_low[h])
            dq[h] = term if dq[h] is None else dq[h] + term
        dv_sum[rows, :] += product(jnp.concatenate(probs_low, axis=1), jnp.concatenate(do_own, axis=0))
        dk_sum[rows, :] += product(jnp.concatenate(grads_low, axis=1), jnp.concatenate(q_own, axis=0))
    dq_ref[...] = (jnp.concatenate(dq, axis=0) * (1.0 / math.sqrt(HEAD))).T.astype(BF)

    @pl.when(i == pl.num_programs(1) - 1)
    def _():
        dk_ref[...] = (dk_sum[...] * (1.0 / math.sqrt(HEAD))).astype(BF)
        dv_ref[...] = dv_sum[...].astype(BF)


def attend_back(q, k, v, starts, heads, q_tags, k_tags, out, lse, grad_out, first=0):
    nq, nk = q.shape[0], k.shape[0]
    pairs = heads // 2
    qb, kb = min(512, nq), min(2048, nk)
    base = first // 2
    q_off, k_off, v_off = (s // PAIR + base for s in starts)
    mine = pl.BlockSpec((qb, PAIR), lambda p, i: (i, p + base))
    return pl.pallas_call(
        functools.partial(attend_back_kernel, kb=kb),
        grid=(pairs, nq // qb),
        in_specs=[
            pl.BlockSpec((qb, PAIR), lambda p, i: (i, q_off + p)),
            pl.BlockSpec((nk, PAIR), lambda p, i: (0, k_off + p)),
            pl.BlockSpec((nk, PAIR), lambda p, i: (0, v_off + p)),
            mine,
            mine,
            pl.BlockSpec((1, 2, qb), lambda p, i: (p + base, 0, i)),
            pl.BlockSpec((qb, PAIR), lambda p, i: (i, 0)),
            pl.BlockSpec((nk, PAIR), lambda p, i: (0, 0)),
        ],
        out_specs=[
            pl.BlockSpec((qb, PAIR), lambda p, i: (i, p)),
            pl.BlockSpec((nk, PAIR), lambda p, i: (0, p)),
            pl.BlockSpec((nk, PAIR), lambda p, i: (0, p)),
        ],
        out_shape=[
            jax.ShapeDtypeStruct((nq, pairs * PAIR), BF),
            jax.ShapeDtypeStruct((nk, pairs * PAIR), BF),
            jax.ShapeDtypeStruct((nk, pairs * PAIR), BF),
        ],
        scratch_shapes=[
            pltpu.VMEM((2, nk, PAIR), BF),
            pltpu.VMEM((PAIR, nk), BF),
            pltpu.VMEM((nk, PAIR), F32),
            pltpu.VMEM((nk, PAIR), F32),
        ],
        compiler_params=kernel_params(),
        cost_estimate=SHORT,
        name="attend_back",
    )(q, k, v, grad_out, out, lse, q_tags, k_tags)


def mlp_up_kernel(a_ref, w_ref, b_ref, hid_ref, slope_ref):
    pre = product(a_ref[...], w_ref[...]) + b_ref[...]
    cdf = 0.5 * (1.0 + lax.erf(pre * (1.0 / math.sqrt(2.0))))
    density = jnp.exp(-0.5 * pre * pre) * (1.0 / math.sqrt(2.0 * math.pi))
    hid_ref[...] = (pre * cdf).astype(BF)
    slope_ref[...] = (cdf + pre * density).astype(BF)


def mlp_up(act, w, bias):
    rows, ff = act.shape[0], w.shape[1]
    cb = 1024
    block = pl.BlockSpec((rows, cb), lambda g: (0, g))
    return pl.pallas_call(
        mlp_up_kernel,
        grid=(ff // cb,),
        in_specs=[
            pl.BlockSpec(act.shape, lambda g: (0, 0)),
            pl.BlockSpec((w.shape[0], cb), lambda g: (0, g)),
            pl.BlockSpec((1, cb), lambda g: (0, g)),
        ],
        out_specs=[block, block],
        out_shape=[jax.ShapeDtypeStruct((rows, ff), BF)] * 2,
        compiler_params=kernel_params(),
        cost_estimate=SHORT,
        name="mlp_up",
    )(act, w, bias)


def mlp_back_kernel(g_ref, w_ref, slope_ref, out_ref, sum_ref):
    grad = product_t(g_ref[...], w_ref[...]) * slope_ref[...].astype(F32)
    low = grad.astype(BF)
    out_ref[...] = low
    sum_ref[...] = jnp.sum(low.astype(F32), axis=0, keepdims=True)


def mlp_back(grad, w, slope):
    rows, ff = slope.shape
    cb = 1024
    block = pl.BlockSpec((rows, cb), lambda g: (0, g))
    return pl.pallas_call(
        mlp_back_kernel,
        grid=(ff // cb,),
        in_specs=[
            pl.BlockSpec(grad.shape, lambda g: (0, 0)),
            pl.BlockSpec((cb, w.shape[1]), lambda g: (g, 0)),
            block,
        ],
        out_specs=[block, pl.BlockSpec((1, cb), lambda g: (0, g))],
        out_shape=[jax.ShapeDtypeStruct((rows, ff), BF), jax.ShapeDtypeStruct((1, ff), F32)],
        compiler_params=kernel_params(),
        cost_estimate=SHORT,
        name="mlp_back",
    )(grad, w, slope)


def norm_parts(values):
    centre = values - jnp.mean(values, axis=-1, keepdims=True)
    spread = jnp.mean(centre * centre, axis=-1, keepdims=True)
    inverse = lax.rsqrt(spread + 1e-05)
    return centre * inverse, inverse


def norm_back(unit, inverse, grad):
    return inverse * (
        grad
        - jnp.mean(grad, axis=-1, keepdims=True)
        - unit * jnp.mean(grad * unit, axis=-1, keepdims=True)
    )


def per_item(ids, rows):
    out = jnp.broadcast_to(rows[0:1, :], (ids.shape[0], rows.shape[1]))
    for n in range(1, rows.shape[0]):
        out = jnp.where(ids == n, rows[n : n + 1, :], out)
    return out


def modulate_kernel(me_ref, *refs, per, offsets):
    pieces, (id_ref, mod_ref, out_ref, x_ref) = refs[:-4], refs[-4:]
    width = out_ref.shape[1]
    block = pl.program_id(0) // per
    for off, piece in zip(offsets, pieces):
        @pl.when(me_ref[0] + off == block)
        def _():
            x_ref[...] = piece[...]

    unit, _ = norm_parts(x_ref[...].astype(F32))
    ids = id_ref[...]
    shift = per_item(ids, mod_ref[:, :width])
    scale = per_item(ids, mod_ref[:, width:])
    out_ref[...] = (unit * (1.0 + scale) + shift).astype(BF)


def modulate(pieces, offsets, me, ids, mod_items):
    rows, width = pieces[0].shape
    rb = min(512, rows)
    per = rows // rb
    total = ids.shape[0]
    block = pl.BlockSpec((rb, width), lambda i, me: (i, 0))
    return pl.pallas_call(
        functools.partial(modulate_kernel, per=per, offsets=offsets),
        grid_spec=pltpu.PrefetchScalarGridSpec(
            num_scalar_prefetch=1,
            grid=(total // rb,),
            in_specs=[
                pl.BlockSpec((rb, width), lambda i, me, off=off: (jnp.where(me[0] + off == i // per, i % per, 0), 0))
                for off in offsets
            ]
            + [
                pl.BlockSpec((rb, 1), lambda i, me: (i, 0)),
                pl.BlockSpec(mod_items.shape, lambda i, me: (0, 0)),
            ],
            out_specs=[block, block],
        ),
        out_shape=[jax.ShapeDtypeStruct((total, width), BF)] * 2,
        compiler_params=kernel_params(),
        cost_estimate=SHORT,
        name="modulate",
    )(me.reshape(1), *pieces, ids, mod_items)


def modulate_back_kernel(dq_ref, dk_ref, dv_ref, w_ref, x_ref, id_ref, out_ref, sum_ref):
    width = x_ref.shape[1]
    c = dq_ref.shape[1]
    items = sum_ref.shape[0]
    grad = product_t(dq_ref[...], w_ref[:, 0:c])
    grad += product_t(dk_ref[...], w_ref[:, c : 2 * c])
    grad += product_t(dv_ref[...], w_ref[:, 2 * c :])
    out_ref[...] = grad.astype(BF)

    @pl.when(pl.program_id(0) == 0)
    def _():
        sum_ref[...] = jnp.zeros(sum_ref.shape, F32)

    unit, _ = norm_parts(x_ref[...].astype(F32))
    times = grad * unit
    ids = id_ref[...]
    low, high = jnp.min(ids), jnp.max(ids)
    for n in range(items):
        @pl.when((low <= n) & (n <= high))
        def _():
            here = ids == n
            sum_ref[n : n + 1, :width] += jnp.sum(jnp.where(here, grad, 0.0), axis=0, keepdims=True)
            sum_ref[n : n + 1, width:] += jnp.sum(jnp.where(here, times, 0.0), axis=0, keepdims=True)


def modulate_back(d_q, d_k, d_v, w, x, ids, items):
    rows, width = x.shape
    rb = 512
    c = d_q.shape[1]
    part = pl.BlockSpec((rb, c), lambda i: (i, 0))
    return pl.pallas_call(
        modulate_back_kernel,
        grid=(rows // rb,),
        in_specs=[
            part,
            part,
            part,
            pl.BlockSpec(w.shape, lambda i: (0, 0)),
            pl.BlockSpec((rb, width), lambda i: (i, 0)),
            pl.BlockSpec((rb, 1), lambda i: (i, 0)),
        ],
        out_specs=[
            pl.BlockSpec((rb, width), lambda i: (i, 0)),
            pl.BlockSpec((items, 2 * width), lambda i: (0, 0)),
        ],
        out_shape=[jax.ShapeDtypeStruct((rows, width), BF), jax.ShapeDtypeStruct((items, 2 * width), F32)],
        compiler_params=kernel_params(),
        cost_estimate=SHORT,
        name="modulate_back",
    )(d_q, d_k, d_v, w, x, ids)


def grads_kernel(*refs, spans, sources, count):
    g = pl.program_id(0)
    x_refs, y_refs, out_ref, xt_ref = refs[:count], refs[count:-2], refs[-2], refs[-1]
    for i, (start, stop) in enumerate(spans):
        rows = y_refs[i].shape[0]
        if i == 0 or sources[i] != sources[i - 1]:
            @pl.when(g == start)
            def _():
                xt_ref[:, :rows] = x_refs[sources[i]][...].T

        @pl.when((g >= start) & (g < stop))
        def _():
            out_ref[...] = product(xt_ref[:, :rows], y_refs[i][...]).astype(BF)


def weight_grads(pairs):
    flat = [(n, y) for n, (_, ys) in enumerate(pairs) for y in ys]
    width = pairs[0][0].shape[1]
    cb = min(1024, min(y.shape[1] for _, y in flat))
    spans, at = [], 0
    for _, y in flat:
        spans.append((at, at + y.shape[1] // cb))
        at = spans[-1][1]
    in_specs = [pl.BlockSpec(x.shape, lambda g: (0, 0), pipeline_mode=pl.Buffered(1)) for x, _ in pairs]
    for (_, y), (start, stop) in zip(flat, spans):
        in_specs.append(
            pl.BlockSpec((y.shape[0], cb), lambda g, start=start, stop=stop: (0, jnp.clip(g - start, 0, stop - start - 1)))
        )
    longest = max(x.shape[0] for x, _ in pairs)
    return pl.pallas_call(
        functools.partial(grads_kernel, spans=tuple(spans), sources=tuple(n for n, _ in flat), count=len(pairs)),
        grid=(at,),
        in_specs=in_specs,
        out_specs=pl.BlockSpec((width, cb), lambda g: (0, g)),
        scratch_shapes=[pltpu.VMEM((width, longest), BF)],
        out_shape=jax.ShapeDtypeStruct((width, at * cb), BF),
        compiler_params=kernel_params(),
        cost_estimate=SHORT,
        name="weight_grads",
    )(*[x for x, _ in pairs], *[y for _, y in flat])


def bits_of(size):
    return [1 << b for b in range(size.bit_length() - 1)]


class Axis:
    def __init__(self, name, length, size, me, flip):
        self.name, self.length, self.size, self.me, self.flip = name, length, size, me, flip

    def send(self, value, m):
        return lax.ppermute(value, self.name, [(r, r ^ self.flip(m)) for r in range(self.length)])

    def mine(self, bit):
        return (self.me // bit) % 2


def pick(value, index, where):
    return lax.dynamic_index_in_dim(value, index, where, keepdims=False)


def sync(*values):
    return lax.optimization_barrier(values)


def natural(pieces, axis):
    pieces = list(pieces)
    for bit in bits_of(axis.size):
        flip = axis.mine(bit) == 1
        out = list(pieces)
        for m in range(axis.size):
            if not m & bit:
                out[m] = jnp.where(flip, pieces[m | bit], pieces[m])
                out[m | bit] = jnp.where(flip, pieces[m], pieces[m | bit])
        pieces = out
    return pieces


def join(pieces, axis):
    if isinstance(pieces, dict):
        pieces = [pieces[m] for m in range(axis.size)]
    return jnp.concatenate(natural(pieces, axis), axis=0)


def exchange_start(blocks, axis):
    return [pick(blocks, axis.me ^ m, 0) if m == 0 else axis.send(pick(blocks, axis.me ^ m, 0), m) for m in range(axis.size)]


def xor_start(value, axis):
    return [value] + [axis.send(value, m) for m in range(1, axis.size)]


def double_start(have, bit, axis):
    return {**have, **{m | bit: axis.send(v, bit) for m, v in have.items()}}


class LineSum:
    def __init__(self, parts, ns):
        self.parts, self.ns, self.k = parts, ns, 0
        self.moved = None

    def chunk(self, d):
        rows = self.parts.shape[0] // self.ns
        return lax.dynamic_slice_in_dim(self.parts, jnp.clip(d, 0, self.ns - 1) * rows, rows).astype(F32)

    def start(self):
        self.k += 1
        k, ns, me = self.k, self.ns, lax.axis_index("seq")
        above, below = self.chunk(me + ns - k), self.chunk(me - ns + k)
        if self.moved is not None:
            above, below = above + self.moved[0].astype(F32), below + self.moved[1].astype(F32)
        self.moved = (
            lax.ppermute(above.astype(BF), "seq", [(r, r + 1) for r in range(k)]),
            lax.ppermute(below.astype(BF), "seq", [(ns - 1 - r, ns - 2 - r) for r in range(k)]),
        )

    def total(self):
        return self.chunk(lax.axis_index("seq")) + self.moved[0].astype(F32) + self.moved[1].astype(F32)


def line_step(up, down, ns):
    return (
        lax.ppermute(up, "seq", [(r, r + 1) for r in range(ns - 1)]),
        lax.ppermute(down, "seq", [(r + 1, r) for r in range(ns - 1)]),
    )


def line_join(ups, downs, ns):
    ring = [ups[0]] + [downs[r] + ups[ns - r] for r in range(1, ns)]
    rows = ups[0].shape[0]
    first = (ns - lax.axis_index("seq")) % ns
    return lax.dynamic_slice_in_dim(jnp.concatenate(ring + ring[:-1], axis=0), first * rows, ns * rows)


def add_all(pieces, dtype=F32):
    total = pieces[0].astype(F32)
    for value in pieces[1:]:
        total = total + value.astype(F32)
    return total.astype(dtype)


def to_dp(whole):
    return lax.psum_scatter(whole, "dp", scatter_dimension=0, tiled=True)


def block(nd, ns, tokens, patches, cameras, tri_items, patch_items, mod_weight, qkv_weight, self_out_weight, norm2_gain, norm2_bias, cross_q_weight, cross_kv_weight, cross_out_weight, norm3_gain, norm3_bias, mlp_in_weight, mlp_in_bias, mlp_out_weight, mlp_out_bias, cotangent):
    rows, width = tokens.shape
    heads_here = HEADS // ns
    cols_here = width // ns
    items = cameras.shape[0]
    w_rows = qkv_weight.shape[0]
    n_dev = nd * ns
    seq = Axis("seq", ns, ns, lax.axis_index("seq"), lambda m: m)

    def over_dp(held):
        return lax.all_gather(join(held, seq), "dp", axis=0, tiled=True)

    down_bits = bits_of(ns)[::-1]

    bundle = {0: jnp.concatenate([self_out_weight, cross_q_weight, cross_kv_weight, cross_out_weight], axis=1)}
    small = jnp.concatenate(
        [mod_weight.reshape(-1), norm2_gain, norm2_bias, norm3_gain, norm3_bias, mlp_out_bias, mlp_in_bias]
    )
    length = small.shape[0]
    extra = -(-length // w_rows)
    extra += -extra % 128
    small = jnp.pad(small, (0, extra * w_rows - length)).reshape(w_rows, extra)
    cut = qkv_weight.reshape(w_rows, 3, ns, cols_here).transpose(2, 0, 1, 3).reshape(ns, w_rows, 3 * cols_here)
    cut = jnp.concatenate([cut, jnp.broadcast_to(small[None], (ns, w_rows, extra))], axis=2)

    ups, downs = [tokens], [tokens]
    todo = list(down_bits)
    for k in range(1, ns):
        up, down = line_step(ups[-1], downs[-1], ns)
        if k == 1:
            cut = exchange_start(cut, seq)
            up, down, cut = sync(up, down, cut)
            cut = lax.all_gather(join(cut, seq), "dp", axis=0, tiled=True)
        else:
            if todo:
                bundle = double_start(bundle, todo.pop(0), seq)
                up, down, bundle = sync(up, down, bundle)
                if not todo:
                    bundle = over_dp(bundle)
            else:
                up, down = sync(up, down)
        ups.append(up)
        downs.append(down)
    if len(todo) or ns == 2:
        while todo:
            bundle = double_start(bundle, todo.pop(0), seq)
        bundle = over_dp(bundle)
    ups, downs, cut, patches, mlp_in_weight = sync(ups, downs, cut, patches, mlp_in_weight)
    qkv_mine = cut[:, : 3 * cols_here]
    small = cut[:, 3 * cols_here :].reshape(n_dev, -1)
    mod_n = mod_weight.size
    own = norm2_gain.shape[0]
    mod_full = small[:, :mod_n].reshape(-1, mod_weight.shape[1])
    vectors = [small[:, mod_n + n * own : mod_n + (n + 1) * own].reshape(1, -1).astype(F32) for n in range(5)]
    gain_two, bias_two, gain_three, bias_three, out_bias = vectors
    in_bias = small[:, mod_n + 5 * own : length].reshape(1, -1).astype(F32)

    tri_col = tri_items.reshape(-1, 1)
    tri_query, tri_key = query_tags(tri_items, items), key_tags(tri_items)
    my_items = lax.dynamic_slice_in_dim(tri_items, seq.me * rows, rows)
    my_query, patch_key = query_tags(my_items, items), key_tags(patch_items)

    mod_items = product_t(cameras, mod_full)
    patch_ups, patch_downs = [patches], [patches]

    def patch_step():
        if len(patch_ups) < ns:
            up, down = line_step(patch_ups[-1], patch_downs[-1], ns)
            patch_ups.append(up)
            patch_downs.append(down)

    patch_step()
    w_in = double_start({0: mlp_in_weight}, down_bits[0], seq)
    steps = range(1, ns)
    act_one, token_all = modulate(
        [tokens] + ups[1:] + downs[1:], [0] + [-k for k in steps] + list(steps), seq.me, tri_col, mod_items
    )
    act_one, w_in, patch_ups[-1], patch_downs[-1] = sync(act_one, w_in, patch_ups[-1], patch_downs[-1])
    for bit in down_bits[1:]:
        w_in = double_start(w_in, bit, seq)
    patch_step()
    qkv = product(act_one, qkv_mine).astype(BF)
    qkv, w_in, mlp_out_weight, patch_ups[-1], patch_downs[-1] = sync(
        qkv, w_in, mlp_out_weight, patch_ups[-1], patch_downs[-1]
    )
    w_in = over_dp(w_in)
    while len(patch_ups) < ns:
        patch_step()
    w_out = double_start({0: mlp_out_weight}, down_bits[0], seq)
    self_at = (0, cols_here, 2 * cols_here)
    self_mine, self_lse = attend(qkv, qkv, qkv, self_at, heads_here, tri_query, tri_key)
    self_mine, bundle, patch_ups, patch_downs, w_out = sync(self_mine, bundle, patch_ups, patch_downs, w_out)
    w_self_out = bundle[:, :width]
    w_cross_q = bundle[:, width : 2 * width]
    w_cross_kv = bundle[:, 2 * width : 4 * width]
    w_cross_out = bundle[:, 4 * width :]
    self_att = lax.all_to_all(self_mine, "seq", 0, 1, tiled=True)
    patch_all = line_join(patch_ups, patch_downs, ns)
    cross_kv = product(patch_all, w_cross_kv).astype(BF)
    self_att, cross_kv = sync(self_att, cross_kv)
    for bit in down_bits[1:]:
        w_out = double_start(w_out, bit, seq)
    resid_in = tokens.astype(F32)
    resid_two = resid_in + product(self_att, w_self_out)

    unit_two, inv_two = norm_parts(resid_two)
    act_two = (unit_two * gain_two + bias_two).astype(BF)
    cross_q = product(act_two, w_cross_q).astype(BF)
    cross_q, w_out = sync(cross_q, w_out)
    w_out = over_dp(w_out)
    cross_at = (0, 0, width)
    cross_att, cross_lse = attend(cross_q, cross_kv, cross_kv, cross_at, HEADS, my_query, patch_key)
    resid_three = resid_two + product(cross_att, w_cross_out)

    unit_three, inv_three = norm_parts(resid_three)
    act_three = (unit_three * gain_three + bias_three).astype(BF)
    act_three, w_in = sync(act_three, w_in)
    hid, slope = mlp_up(act_three, w_in, in_bias)

    g_w_out = contract_rows(hid, cotangent).astype(BF)
    slope, g_w_out, w_out = sync(slope, g_w_out, w_out)
    g_w_out = to_dp(g_w_out)
    grad_out = cotangent.astype(F32)
    g_out_bias = jnp.sum(grad_out, axis=0)
    d_pre, g_in_bias = mlp_back(cotangent, w_out, slope)
    g_w_in = contract_rows(act_three, d_pre).astype(BF)
    d_pre, g_w_in = sync(d_pre, g_w_in)
    g_w_in = to_dp(g_w_in)
    d_act_three = product_t(d_pre, w_in)
    g_gain_three = jnp.sum(d_act_three * unit_three, axis=0)
    g_bias_three = jnp.sum(d_act_three, axis=0)
    d_resid_three = grad_out + norm_back(unit_three, inv_three, d_act_three * gain_three)

    d_cross_out = d_resid_three.astype(BF)
    d_cross = product_t(d_cross_out, w_cross_out).astype(BF)
    d_cq, d_ck, d_cv = attend_back(
        cross_q, cross_kv, cross_kv, cross_at, HEADS, my_query, patch_key, cross_att, cross_lse, d_cross
    )
    d_act_two = product_t(d_cq, w_cross_q)
    g_gain_two = jnp.sum(d_act_two * unit_two, axis=0)
    g_bias_two = jnp.sum(d_act_two, axis=0)
    d_resid_two = d_resid_three + norm_back(unit_two, inv_two, d_act_two * gain_two)

    d_self_out = d_resid_two.astype(BF)
    d_self = product_t(d_self_out, w_self_out).astype(BF)
    d_self_mine = lax.all_to_all(d_self, "seq", 1, 0, tiled=True)

    def over_seq(value):
        return exchange_start(value.reshape((ns, -1) + value.shape[1:]), seq)

    g_mid = weight_grads(
        [(self_att, [d_self_out]), (act_two, [d_cq]), (patch_all, [d_ck, d_cv]), (cross_att, [d_cross_out])]
    )
    patch_part = (product_t(d_ck, w_cross_kv[:, :width]) + product_t(d_cv, w_cross_kv[:, width:])).astype(BF)
    d_self_mine, g_mid, patch_part, g_w_out = sync(d_self_mine, g_mid, patch_part, g_w_out)
    g_mid = to_dp(g_mid)
    out_sum, in_sum = over_seq(g_w_out), None
    patch_line = LineSum(patch_part, ns)
    patch_line.start()
    backs = []
    for first in range(0, heads_here, 2):
        back = attend_back(
            qkv, qkv, qkv, self_at, 2, tri_query, tri_key, self_mine, self_lse, d_self_mine, first=first
        )
        if in_sum is None:
            back, d_self_mine, g_w_in, patch_line.moved = sync(back, d_self_mine, g_w_in, patch_line.moved)
            in_sum = over_seq(g_w_in)
            patch_line.start()
        backs.append(back)
    backs, patch_line.moved, out_sum, in_sum = sync(backs, patch_line.moved, out_sum, in_sum)
    for _ in range(patch_line.k, ns - 1):
        patch_line.start()
    d_q, d_k, d_v = (jnp.concatenate(p, axis=1) if len(p) > 1 else p[0] for p in zip(*backs))
    d_act_one, g_mod_items = modulate_back(d_q, d_k, d_v, qkv_mine, token_all, tri_col, items)
    d_act_one, g_mod_items, d_q, d_k, d_v, in_sum, patch_line.moved, out_sum = sync(
        d_act_one, g_mod_items, d_q, d_k, d_v, in_sum, patch_line.moved, out_sum
    )

    line = LineSum(d_act_one, ns)
    line.start()
    g_mod = lax.dot_general(
        g_mod_items, cameras.astype(F32), (((0,), (0,)), ((), ())), precision=lax.Precision.HIGHEST
    )
    tail = jnp.concatenate(
        [g_mod.reshape(n_dev, -1)]
        + [v.reshape(n_dev, -1) for v in (g_gain_two, g_bias_two, g_gain_three, g_bias_three, g_out_bias, g_in_bias)],
        axis=1,
    )
    tail = jnp.pad(tail, ((0, 0), (0, extra * w_rows - length))).reshape(n_dev * w_rows, extra).astype(BF)
    g_qkv = weight_grads([(act_one, [d_q, d_k, d_v])])
    g_qkv = jnp.concatenate([g_qkv, tail], axis=1)
    g_qkv, in_sum, g_mid = sync(g_qkv, in_sum, g_mid)
    g_mid = over_seq(g_mid)
    line.moved, g_qkv, g_mid[1], hid = sync(line.moved, g_qkv, g_mid[1], hid)
    g_qkv = to_dp(g_qkv)
    line.start()
    g_mid[2], hid, patch_line.moved, out_sum, in_sum = sync(g_mid[2], hid, patch_line.moved, out_sum, in_sum)
    block_out = (resid_three + product(hid, w_out) + out_bias).astype(BF)
    patch_grad, g_w_out, g_w_in = patch_line.total(), add_all(out_sum), add_all(in_sum)
    line.moved, patch_grad, g_w_out, g_w_in, g_mid, block_out = sync(
        line.moved, patch_grad, g_w_out, g_w_in, g_mid, block_out
    )
    for _ in range(line.k, ns - 1):
        line.start()
    g_mid = add_all(g_mid)
    line.moved, g_mid, g_qkv = sync(line.moved, g_mid, g_qkv)
    g_qkv = exchange_start(g_qkv.reshape(ns, w_rows, -1), seq)
    d_act_one = line.total()
    unit_own, inv_own = norm_parts(resid_in)
    scale_own = per_item(my_items.reshape(-1, 1), mod_items[:, width:])
    input_grad = d_resid_two + norm_back(unit_own, inv_own, d_act_one * (1.0 + scale_own))
    g_qkv = join([g[None] for g in g_qkv], seq).astype(F32)
    tail = jnp.sum(g_qkv[:, :, 3 * cols_here :], axis=0).reshape(-1)
    g_mod = tail[:mod_n].reshape(mod_weight.shape)
    parts = [tail[mod_n + n * own : mod_n + (n + 1) * own] for n in range(5)]
    g_in_bias = tail[mod_n + 5 * own : length]
    g_qkv = g_qkv[:, :, : 3 * cols_here].reshape(ns, w_rows, 3, cols_here)
    g_qkv = g_qkv.transpose(1, 2, 0, 3).reshape(qkv_weight.shape)
    return (
        block_out,
        input_grad,
        patch_grad,
        g_mod,
        g_qkv,
        g_mid[:, :width],
        parts[0],
        parts[1],
        g_mid[:, width : 2 * width],
        g_mid[:, 2 * width : 4 * width],
        g_mid[:, 4 * width :],
        parts[2],
        parts[3],
        g_w_in,
        g_in_bias,
        g_w_out,
        parts[4],
    )


def solution(mesh):
    nd, ns = mesh.shape["dp"], mesh.shape["seq"]
    rows2, rows1 = P(ALL, None), P(ALL)
    placed = (rows2, rows2, P("dp", None), P("dp"), P("dp"), rows2, rows2, rows2, rows1, rows1, rows2, rows2, rows2, rows1, rows1, rows2, rows1, rows2, rows1, rows2)
    given = (rows2, rows2, rows2, rows2, rows2, rows2, rows1, rows1, rows2, rows2, rows2, rows1, rows1, rows2, rows1, rows2, rows1)

    def shards(*args):
        return block(nd, ns, *args)

    return jax.shard_map(shards, mesh=mesh, in_specs=placed, out_specs=given, check_vma=False)
```
